32 devices in a mesh: clips: 2 (over y), tok: 4 (over z), head: 4 (over x, core).
Axes of the slice: x: 2, y: 2, z: 4, core: 2. Of those that a mesh axis runs over, the one named last changes fastest.
Arguments:
- query: bfloat16 [24, 256, 1536], P(('clips', 'tok'), 'head'), parts along dimension 0, may hold values from -16 to 16, as said below
- key: bfloat16 [24, 256, 1536], P(('clips', 'tok'), 'head'), parts along dimension 0, may hold values from -16 to 16
- value: bfloat16 [24, 256, 1536], P(('clips', 'tok'), 'head'), parts along dimension 0, may hold values from -6 to 6
- valid_rows: int32 [24], P(('clips', 'tok')), parts along dimension 0, may hold values from 1 to 8, as said below
Outputs:
- attended: bfloat16 [24, 256, 1536], P(('clips', 'tok'), 'head'), parts along dimension 0
The draws below stay inside these ranges and needn't reach their ends.
There are 2 independent parts, one for each index of `clips`. The reference program is written for one: setup_inputs(seed, part) draws one part's arguments, and reference() takes and returns one part's arrays. A program takes and returns all parts, laid end to end along the dimension named above; each array names one. Nothing has to cross between parts.
Inputs may be any that keep to these rules, and one draw needn't show every extreme that they name: Entries of query and key lie within -16 and 16. `valid_rows`: tiles outside the last height-tile row have all 8 rows real; tiles of the last height-tile row each have their own count.
All inputs are finite; a program needn't handle non-finite values.
Results may differ from the reference program's by a relative error of at most 0.0031.
Values may be sent and summed in bfloat16 or wider, within the bound.
No kernel may reach another device: no remote copies, remote signals or barrier semaphores. Data moves between devices by JAX's collectives and lax.ppermute only.
A program may use at most 64 MiB of HBM per device.

```python
import math
import jax
import jax.numpy as jnp
from jax import lax

HEADS = 12
HEAD_DIM = 128
TILE_H = 8
TILE_W = 8
TIME_TILES = 4
WIDTH_TILES = 3
HEIGHT_TILES = 1
TILE = 256
TILES = 12


def pair_fields(key):
    shape = (TILES, TILE, HEADS * HEAD_DIM)
    base_q = 1.6 * jnp.clip(jax.random.normal(jax.random.fold_in(key, 11), shape, jnp.float32), -4.0, 4.0)
    base_k = 1.6 * jnp.clip(jax.random.normal(jax.random.fold_in(key, 12), shape, jnp.float32), -4.0, 4.0)
    return (base_q, base_k)


def draw_query(key, part):
    return pair_fields(key)[0].astype(jnp.bfloat16)


def draw_key(key, part):
    return pair_fields(key)[1].astype(jnp.bfloat16)


def draw_valid_rows(key, part):
    tile_id = jnp.arange(TILES)
    random_counts = jax.random.randint(jax.random.fold_in(key, 21), (TILES,), 1, TILE_H + 1)
    height_pos = tile_id // WIDTH_TILES % HEIGHT_TILES
    time_pos = tile_id // (WIDTH_TILES * HEIGHT_TILES)
    bottom = height_pos == HEIGHT_TILES - 1
    bottom_counts = jnp.where(time_pos == 1, TILE_H, jnp.where(time_pos == 2, 1, random_counts))
    rows = jnp.where(bottom, bottom_counts, TILE_H)
    return rows.astype(jnp.int32)


def block_scale(rng, shape, pieces, low, high):
    gain, own = 1.0, jax.random.fold_in(rng, 6)
    for dim, blocks in pieces:
        steps = jnp.exp(jax.random.uniform(jax.random.fold_in(own, dim), (blocks,), jnp.float32, low / len(pieces), high / len(pieces)))
        gain = gain * jnp.repeat(steps, shape[dim] // blocks).reshape([-1 if axis == dim else 1 for axis in range(len(shape))])
    return gain


def scatter_about(stream_key, shape, deviation, bound, pieces=(), kind=jnp.bfloat16):
    array = jax.random.normal(stream_key, shape, jnp.float32) * deviation
    if len(pieces) > 0:
        array = block_scale(stream_key, shape, pieces, -0.22, 0.18) * array
    return jnp.clip(array, min=-bound, max=bound).astype(kind)


def setup_inputs(seed: int = 0, part: int = 0) -> dict:
    key_list = jax.random.split(jax.random.key(seed), 5)
    part_splits = jax.random.split(jax.random.fold_in(key_list[4], part), 5)
    query = draw_query(jax.random.fold_in(jax.random.fold_in(key_list[4], part), 71), part)
    key = draw_key(jax.random.fold_in(jax.random.fold_in(key_list[4], part), 71), part)
    value = scatter_about(part_splits[2], (TILES, TILE, HEADS * HEAD_DIM), 1.0, 6.0, ((0, 4), (1, 4)))
    valid_rows = draw_valid_rows(jax.random.fold_in(jax.random.fold_in(key_list[4], part), 71), part)
    return {"query": query, "key": key, "value": value, "valid_rows": valid_rows}


def reference(query, key, value, valid_rows):
    grid = (TIME_TILES, HEIGHT_TILES, WIDTH_TILES)
    scale = 1.0 / math.sqrt(HEAD_DIM)

    def per_head(field):
        return jnp.moveaxis(field.reshape(grid + (TILE, HEADS, HEAD_DIM)), 4, 0)
    counts = jnp.pad(valid_rows.reshape(grid), 1)
    count_win = jnp.stack([counts[a:a + TIME_TILES, b:b + HEIGHT_TILES, c:c + WIDTH_TILES] for a in range(3) for b in range(3) for c in range(3)], axis=-1)
    row_index = jnp.arange(TILE) // TILE_W % TILE_H
    mask = (row_index[None, None, None, None, :] < count_win[..., None]).reshape(grid + (27 * TILE,))

    def window(field):
        padded = jnp.pad(field, ((1, 1), (1, 1), (1, 1), (0, 0), (0, 0)))
        parts = [padded[a:a + TIME_TILES, b:b + HEIGHT_TILES, c:c + WIDTH_TILES] for a in range(3) for b in range(3) for c in range(3)]
        return jnp.stack(parts, axis=3).reshape(grid + (27 * TILE, HEAD_DIM))

    def one_head(items):
        q_head, k_head, v_head = items
        k_win = window(k_head)
        v_win = window(v_head)

        def one_time(inner):
            q_part, k_part, v_part, m_part = inner
            scores = jnp.einsum('bcqd,bckd->bcqk', q_part.astype(jnp.float32), k_part.astype(jnp.float32)) * scale
            scores = jnp.where(m_part[:, :, None, :], scores, -jnp.inf)
            largest = lax.optimization_barrier(jnp.max(scores, axis=-1, keepdims=True))
            weight = jnp.exp(scores - largest)
            total = lax.optimization_barrier(jnp.sum(weight, axis=-1, keepdims=True))
            rounded = weight.astype(jnp.bfloat16)
            summed = jnp.einsum('bcqk,bckd->bcqd', rounded.astype(jnp.float32), v_part.astype(jnp.float32))
            return (summed / total).astype(jnp.bfloat16)
        return lax.map(one_time, (q_head, k_win, v_win, mask))
    result = lax.map(one_head, (per_head(query), per_head(key), per_head(value)))
    result = jnp.moveaxis(result, 0, 4)
    return result.reshape(TILES, TILE, HEADS * HEAD_DIM)
```

```python
import functools
import math

import jax
import jax.numpy as jnp
from jax import lax
from jax.experimental import pallas as pl
from jax.experimental.pallas import tpu as pltpu
from jax.sharding import PartitionSpec as P

HEAD_DIM = 128
TILE_H = 8
TILE_W = 8
TIME_TILES = 4
COUNT_ROWS = 16
MASKED = -1e30
VMEM_LIMIT = 48 * 2**20


def in_vmem(count):
    return [pl.BlockSpec(memory_space=pltpu.VMEM)] * count


def anywhere(count):
    return [pl.BlockSpec(memory_space=pl.ANY)] * count


def swap_head(block, bit, devices):
    return lax.ppermute(block, "head", [(i, i ^ bit) for i in range(devices)])


def swap_pairs(block, phase, stride, length, devices):
    route = []
    for i in range(devices):
        place = i // stride % length
        if place % 2 == phase and place + 1 < length:
            route += [(i, i + stride), (i + stride, i)]
    return lax.ppermute(block, "tok", route)


def pack_body(devices, part, me_ref, counts_ref, q_ref, k_ref, v_ref, *rest):
    near_ref, sibling_ref, own_q_ref = rest[:3]
    far_refs, far_q_refs = rest[3 : 1 + devices], rest[1 + devices : 2 * devices - 1]
    counts_buf, sems = rest[2 * devices - 1 :]
    rows = k_ref.shape[0]
    me = me_ref[0]

    def lanes(bit):
        return pl.ds(pl.multiple_of((me ^ bit) * part, HEAD_DIM), part)

    jobs = [
        (k_ref.at[:, lanes(0)], near_ref.at[pl.ds(0, rows)]),
        (v_ref.at[:, lanes(0)], near_ref.at[pl.ds(rows, rows)]),
        (k_ref.at[:, lanes(1)], near_ref.at[pl.ds(2 * rows + COUNT_ROWS, rows)]),
        (v_ref.at[:, lanes(1)], near_ref.at[pl.ds(3 * rows + COUNT_ROWS, rows)]),
        (k_ref.at[:, lanes(1)], sibling_ref.at[pl.ds(0, rows)]),
        (v_ref.at[:, lanes(1)], sibling_ref.at[pl.ds(rows, rows)]),
        (q_ref.at[:, lanes(1)], sibling_ref.at[pl.ds(2 * rows, rows)]),
        (q_ref.at[:, lanes(0)], own_q_ref),
    ]
    for bit in range(2, devices):
        jobs += [
            (k_ref.at[:, lanes(bit)], far_refs[bit - 2].at[pl.ds(0, rows)]),
            (v_ref.at[:, lanes(bit)], far_refs[bit - 2].at[pl.ds(rows, rows)]),
            (q_ref.at[:, lanes(bit)], far_q_refs[bit - 2]),
        ]
    copies = [pltpu.make_async_copy(src, dst, sems.at[i]) for i, (src, dst) in enumerate(jobs)]
    for copy in copies:
        copy.start()
    row = lax.broadcasted_iota(jnp.int32, counts_buf.shape, 0)
    filled = jnp.zeros(counts_buf.shape, jnp.float32)
    for tile in range(counts_ref.shape[0]):
        filled = jnp.where(row == tile, counts_ref[tile].astype(jnp.float32), filled)
    counts_buf[...] = filled.astype(jnp.bfloat16)
    last = pltpu.make_async_copy(
        counts_buf, near_ref.at[pl.ds(2 * rows, COUNT_ROWS)], sems.at[len(jobs)]
    )
    last.start()
    for copy in copies:
        copy.wait()
    last.wait()


def pack(me, counts, query, key, value, devices):
    rows, width = query.shape
    part = width // devices
    far = devices - 2

    def shape(count):
        return jax.ShapeDtypeStruct((count, part), jnp.bfloat16)

    outs = [shape(4 * rows + COUNT_ROWS), shape(3 * rows), shape(rows)]
    outs += [shape(2 * rows)] * far + [shape(rows)] * far
    results = pl.pallas_call(
        functools.partial(pack_body, devices, part),
        out_shape=outs,
        in_specs=[pl.BlockSpec(memory_space=pltpu.SMEM)] * 2 + anywhere(3),
        out_specs=anywhere(len(outs)),
        scratch_shapes=[
            pltpu.VMEM((COUNT_ROWS, part), jnp.bfloat16),
            pltpu.SemaphoreType.DMA((9 + 3 * far,)),
        ],
        cost_estimate=pl.CostEstimate(flops=0, bytes_accessed=4 * query.size * 4, transcendentals=0),
    )(me, counts, query, key, value)
    return results[0], results[1], results[2], results[3 : 3 + far], results[3 + far :]


def attend_body(slots, frames, tiles, tokens, heads, *refs):
    rows = tiles * tokens
    queries = refs[:frames]
    fields = refs[frames : frames + slots * frames]
    outs = refs[frames + slots * frames :]
    scale = math.log2(math.e) / math.sqrt(HEAD_DIM)
    lane = lax.broadcasted_iota(jnp.int32, (1, HEAD_DIM), 1)
    row = (lane // TILE_W % TILE_H).astype(jnp.float32)
    bias = {}
    for slot in range(slots):
        counted = fields[slot * frames][pl.ds(2 * rows, COUNT_ROWS), pl.ds(0, HEAD_DIM)]
        counted = counted.astype(jnp.float32)
        for tile in range(tiles):
            part = jnp.where(row < counted[tile : tile + 1], 0.0, MASKED)
            bias[slot, tile] = jnp.concatenate([part] * (frames * tokens // HEAD_DIM), 1)

    def piece(slot, frame, which, tile, lanes):
        ref = fields[slot * frames + frame]
        base = 2 * rows + COUNT_ROWS if frame == 1 and slot > 0 else 0
        return ref[pl.ds(base + which * rows + tile * tokens, tokens), lanes]

    for head in range(heads):
        lanes = pl.ds(head * HEAD_DIM, HEAD_DIM)
        for tile in range(tiles):
            window = [
                (slot, near)
                for near in range(max(tile - 1, 0), min(tile + 2, tiles))
                for slot in range(slots)
            ]
            members = [(slot, frame, near) for slot, near in window for frame in range(frames)]
            keys = jnp.concatenate([piece(s, f, 0, n, lanes) for s, f, n in members], 0)
            values = jnp.concatenate([piece(s, f, 1, n, lanes) for s, f, n in members], 0)
            asked = jnp.concatenate(
                [ref[pl.ds(tile * tokens, tokens), lanes] for ref in queries], 0
            )
            scores = lax.dot_general(
                asked, keys, (((1,), (1,)), ((), ())), preferred_element_type=jnp.float32
            )
            scores = scores + jnp.concatenate([bias[w] for w in window], 1)
            largest = jnp.max(scores, axis=1, keepdims=True)
            weight = jnp.exp2((scores - largest) * scale)
            total = jnp.sum(weight, axis=1, keepdims=True)
            summed = jnp.dot(
                weight.astype(jnp.bfloat16), values, preferred_element_type=jnp.float32
            )
            result = (summed / total).astype(jnp.bfloat16)
            for frame in range(frames):
                outs[frame][pl.ds(tile * tokens, tokens), lanes] = result[
                    frame * tokens : (frame + 1) * tokens
                ]


def attend(queries, slots, tiles, tokens, heads):
    frames = len(queries)
    fields = [member for slot in slots for member in slot]
    pairs = heads * (3 * tiles - 2) * len(slots) * (frames * tokens) ** 2
    return pl.pallas_call(
        functools.partial(attend_body, len(slots), frames, tiles, tokens, heads),
        out_shape=[jax.ShapeDtypeStruct((tiles * tokens, heads * HEAD_DIM), jnp.bfloat16)] * frames,
        in_specs=in_vmem(frames + len(fields)),
        out_specs=in_vmem(frames),
        compiler_params=pltpu.CompilerParams(vmem_limit_bytes=VMEM_LIMIT),
        cost_estimate=pl.CostEstimate(
            flops=4 * HEAD_DIM * pairs, bytes_accessed=0, transcendentals=pairs
        ),
    )(*queries, *fields)


def join_body(devices, part, me_ref, *rest):
    out_ref, sems = rest[devices], rest[devices + 1]
    me = me_ref[0]
    copies = [
        pltpu.make_async_copy(
            rest[bit],
            out_ref.at[:, pl.ds(pl.multiple_of((me ^ bit) * part, HEAD_DIM), part)],
            sems.at[bit],
        )
        for bit in range(devices)
    ]
    for copy in copies:
        copy.start()
    for copy in copies:
        copy.wait()


def join(me, pieces):
    devices = len(pieces)
    rows, part = pieces[0].shape
    return pl.pallas_call(
        functools.partial(join_body, devices, part),
        out_shape=jax.ShapeDtypeStruct((rows, devices * part), jnp.bfloat16),
        in_specs=[pl.BlockSpec(memory_space=pltpu.SMEM)] + anywhere(devices),
        out_specs=pl.BlockSpec(memory_space=pl.ANY),
        scratch_shapes=[pltpu.SemaphoreType.DMA((devices,))],
    )(me, *pieces)


def body(query, key, value, valid_rows):
    devices = lax.axis_size("head")
    columns = lax.axis_size("tok")
    height = columns // TIME_TILES
    tiles, tokens, width = query.shape
    heads = width // HEAD_DIM // devices
    me = lax.axis_index("head").astype(jnp.int32).reshape(1)
    flat = [field.reshape(tiles * tokens, width) for field in (query, key, value)]
    near, sibling, own_query, far, far_query = pack(me, valid_rows, *flat, devices)

    far = [swap_head(block, bit, devices) for bit, block in enumerate(far, 2)]
    base = [near] + far
    slots = [base]
    if height > 1:
        slots += [[swap_pairs(b, phase, 1, height, columns) for b in base] for phase in (0, 1)]
    slots += [
        [swap_pairs(b, phase, height, TIME_TILES, columns) for b in slot]
        for phase in (0, 1)
        for slot in slots
    ]
    sibling = swap_head(sibling, 1, devices)
    far_query = [swap_head(block, bit, devices) for bit, block in enumerate(far_query, 2)]
    queries = [own_query, sibling[2 * tiles * tokens :], *far_query]
    beside = [sibling] + [swap_head(slot[0], 1, devices) for slot in slots[1:]]
    slots = [[slot[0], other, *slot[1:]] for slot, other in zip(slots, beside)]

    pieces = attend(queries, slots, tiles, tokens, heads)
    pieces = [pieces[0]] + [
        swap_head(piece, bit, devices) for bit, piece in enumerate(pieces[1:], 1)
    ]
    return join(me, pieces).reshape(tiles, tokens, width)


def solution(mesh):
    placed = (
        P(("clips", "tok"), "head", None),
        P(("clips", "tok"), "head", None),
        P(("clips", "tok"), "head", None),
        P(("clips", "tok")),
    )
    return jax.shard_map(
        body,
        mesh=mesh,
        in_specs=placed,
        out_specs=P(("clips", "tok"), "head", None),
        check_vma=False,
    )
```

```python
import functools
import math

import jax
import jax.numpy as jnp
from jax import lax
from jax.experimental import pallas as pl
from jax.experimental.pallas import tpu as pltpu
from jax.sharding import PartitionSpec as P

HEAD_DIM = 128
TILE_H = 8
TILE_W = 8
TIME_TILES = 4
COUNT_ROWS = 16
MASKED = -1e30
VMEM_LIMIT = 24 * 2**20


def in_vmem(count):
    return [pl.BlockSpec(memory_space=pltpu.VMEM)] * count


def swap_head(block, bit, devices):
    return lax.ppermute(block, "head", [(i, i ^ bit) for i in range(devices)])


def swap_pairs(block, phase, stride, length, devices):
    route = []
    for i in range(devices):
        place = i // stride % length
        if place % 2 == phase and place + 1 < length:
            route += [(i, i + stride), (i + stride, i)]
    return lax.ppermute(block, "tok", route)


def pack_body(devices, part, counts_in, me_ref, q_ref, k_ref, v_ref, *rest):
    own_ref, sibling_ref, own_q_ref = rest[:3]
    far_refs, far_q_refs = rest[3 : 1 + devices], rest[1 + devices : 2 * devices - 1]
    counts_ref, count_sem, sems = rest[2 * devices - 1 :]
    rows = k_ref.shape[0]
    me = me_ref[0]

    def lanes(bit):
        return pl.ds(pl.multiple_of((me ^ bit) * part, HEAD_DIM), part)

    count_copy = pltpu.make_async_copy(counts_in, counts_ref, count_sem)
    count_copy.start()
    jobs = []
    for bit, ref in [(1, sibling_ref), *enumerate(far_refs, 2), (0, own_ref)]:
        jobs += [
            (k_ref.at[:, lanes(bit)], ref.at[pl.ds(0, rows)]),
            (v_ref.at[:, lanes(bit)], ref.at[pl.ds(rows, rows)]),
        ]
    jobs += [
        (q_ref.at[:, lanes(1)], sibling_ref.at[pl.ds(2 * rows, rows)]),
        (q_ref.at[:, lanes(0)], own_q_ref),
    ]
    jobs += [(q_ref.at[:, lanes(bit)], ref) for bit, ref in enumerate(far_q_refs, 2)]
    copies = [pltpu.make_async_copy(src, dst, sems.at[i]) for i, (src, dst) in enumerate(jobs)]
    for copy in copies:
        copy.start()
    count_copy.wait()
    shape = (COUNT_ROWS, part)
    row = lax.broadcasted_iota(jnp.int32, shape, 0)
    filled = jnp.zeros(shape, jnp.float32)
    for tile in range(counts_ref.shape[0]):
        filled = jnp.where(row == tile, counts_ref[tile].astype(jnp.float32), filled)
    own_ref[pl.ds(2 * rows, COUNT_ROWS), :] = filled.astype(jnp.bfloat16)
    for copy in copies:
        copy.wait()


def pack(me, counts, query, key, value, devices):
    rows, width = query.shape
    part = width // devices
    far = devices - 2
    sizes = [2 * rows + COUNT_ROWS, 3 * rows, rows] + [2 * rows] * far + [rows] * far
    fields = [pltpu.with_memory_space_constraint(f, pltpu.HBM) for f in (query, key, value)]
    results = pl.pallas_call(
        functools.partial(pack_body, devices, part),
        out_shape=[pltpu.VMEM((size, part), jnp.bfloat16) for size in sizes],
        in_specs=[pl.BlockSpec(memory_space=pltpu.HBM), pl.BlockSpec(memory_space=pltpu.SMEM)]
        + [pl.BlockSpec(memory_space=pltpu.HBM)] * 3,
        out_specs=in_vmem(len(sizes)),
        scratch_shapes=[
            pltpu.SMEM(counts.shape, jnp.int32),
            pltpu.SemaphoreType.DMA,
            pltpu.SemaphoreType.DMA((3 * devices,)),
        ],
        compiler_params=pltpu.CompilerParams(vmem_limit_bytes=VMEM_LIMIT),
        cost_estimate=pl.CostEstimate(flops=0, bytes_accessed=12 * query.size, transcendentals=0),
    )(pltpu.with_memory_space_constraint(counts, pltpu.HBM), me, *fields)
    return results[0], results[1], results[2], results[3 : 3 + far], results[3 + far :]


def stack_body(sizes, *refs):
    blocks, out_ref, sems = refs[:-2], refs[-2], refs[-1]
    copies = [
        pltpu.make_async_copy(
            block.at[pl.ds(0, size)], out_ref.at[pl.ds(sum(sizes[:i]), size)], sems.at[i]
        )
        for i, (block, size) in enumerate(zip(blocks, sizes))
    ]
    for copy in copies:
        copy.start()
    for copy in copies:
        copy.wait()


def stack(blocks, sizes):
    width = blocks[0].shape[1]
    return pl.pallas_call(
        functools.partial(stack_body, sizes),
        out_shape=pltpu.VMEM((sum(sizes), width), jnp.bfloat16),
        in_specs=in_vmem(len(blocks)),
        out_specs=pl.BlockSpec(memory_space=pltpu.VMEM),
        scratch_shapes=[pltpu.SemaphoreType.DMA((len(blocks),))],
        compiler_params=pltpu.CompilerParams(vmem_limit_bytes=VMEM_LIMIT),
        cost_estimate=pl.CostEstimate(
            flops=0, bytes_accessed=sum(sizes) * width, transcendentals=0
        ),
    )(*blocks)


def bias_of(counts, tiles, tokens, copies):
    lane = lax.broadcasted_iota(jnp.int32, (1, HEAD_DIM), 1)
    row = (lane // TILE_W % TILE_H).astype(jnp.float32)
    counted = counts.astype(jnp.float32)
    rows = [jnp.where(row < counted[n : n + 1], 0.0, MASKED) for n in range(tiles)]
    return [jnp.concatenate([r] * (copies * tokens // HEAD_DIM), 1) for r in rows]


def attend_body(groups, operands, frames, tiles, tokens, heads, first, early, *refs):
    rows = tiles * tokens
    refs = list(refs)
    queries = [refs.pop(0) for _ in range(frames)]
    arrays = [refs.pop(0) for _ in range(operands)]
    biases = []
    for counts, fields in groups:
        counted = arrays[counts][pl.ds(2 * rows, COUNT_ROWS), pl.ds(0, HEAD_DIM)]
        biases.append(bias_of(counted, tiles, tokens, len(fields)))
    outs = refs if early else refs[3:]
    scale = math.log2(math.e) / math.sqrt(HEAD_DIM)
    block = frames * tokens

    for head in range(heads):
        lanes = pl.ds((first + head) * HEAD_DIM, HEAD_DIM)
        for tile in range(tiles):
            window = [
                (group, near)
                for near in range(max(tile - 1, 0), min(tile + 2, tiles))
                for group in range(len(groups))
            ]

            def gathered(which):
                return jnp.concatenate(
                    [
                        arrays[i][pl.ds(base + which * rows + near * tokens, tokens), lanes]
                        for group, near in window
                        for i, base in groups[group][1]
                    ],
                    0,
                )

            asked = jnp.concatenate([ref[pl.ds(tile * tokens, tokens), lanes] for ref in queries], 0)
            scores = lax.dot_general(
                asked, gathered(0), (((1,), (1,)), ((), ())), preferred_element_type=jnp.float32
            )
            scores = scores + jnp.concatenate([biases[group][near] for group, near in window], 1)
            largest = jnp.max(scores, axis=1, keepdims=True)
            place = pl.ds(((first + head) * tiles + tile) * block, block)
            if not early:
                before = refs[0][place, :]
                largest = jnp.maximum(before[:, :1], largest)
                shrink = jnp.exp2((before - largest) * scale)
            weight = jnp.exp2((scores - largest) * scale)
            total = jnp.sum(weight, axis=1, keepdims=True)
            summed = jnp.dot(
                weight.astype(jnp.bfloat16), gathered(1), preferred_element_type=jnp.float32
            )
            if early:
                outs[0][place, :] = jnp.broadcast_to(largest, (block, HEAD_DIM))
                outs[1][place, :] = jnp.broadcast_to(total, (block, HEAD_DIM))
                outs[2][place, :] = summed
                continue
            total = total + refs[1][place, :] * shrink
            summed = summed + refs[2][place, :] * shrink
            result = (summed / total).astype(jnp.bfloat16)
            for frame in range(frames):
                outs[frame][pl.ds(tile * tokens, tokens), pl.ds(head * HEAD_DIM, HEAD_DIM)] = result[
                    frame * tokens : (frame + 1) * tokens
                ]


def attend(queries, arrays, groups, tiles, tokens, heads, first=0, state=(), weigh=1):
    frames = len(queries)
    operands = [*queries, *arrays, *state]
    size = sum(len(fields) for _, fields in groups)
    pairs = heads * (3 * tiles - 2) * size * tokens * frames * tokens
    if state:
        outs = [pltpu.VMEM((tiles * tokens, heads * HEAD_DIM), jnp.bfloat16)] * frames
    else:
        left = (heads * tiles * frames * tokens, HEAD_DIM)
        outs = [pltpu.VMEM(left, jnp.float32)] * 3
    return pl.pallas_call(
        functools.partial(
            attend_body, groups, len(arrays), frames, tiles, tokens, heads, first, not state
        ),
        out_shape=outs,
        in_specs=in_vmem(len(operands)),
        out_specs=in_vmem(len(outs)),
        compiler_params=pltpu.CompilerParams(vmem_limit_bytes=VMEM_LIMIT),
        cost_estimate=pl.CostEstimate(
            flops=weigh * 4 * HEAD_DIM * pairs, bytes_accessed=0, transcendentals=weigh * pairs
        ),
    )(*operands)


def join_body(devices, sizes, me_ref, *rest):
    out_ref, sems = rest[-2:]
    me = me_ref[0]
    copies = []
    for part, size in enumerate(sizes):
        for bit in range(devices):
            start = (me ^ bit) * sum(sizes) + sum(sizes[:part])
            copies.append(
                pltpu.make_async_copy(
                    rest[len(copies)],
                    out_ref.at[:, pl.ds(pl.multiple_of(start, HEAD_DIM), size)],
                    sems.at[len(copies)],
                )
            )
    for copy in copies:
        copy.start()
    for copy in copies:
        copy.wait()


def join(me, pieces):
    devices = len(pieces[0])
    rows = pieces[0][0].shape[0]
    sizes = [part[0].shape[1] for part in pieces]
    flat = [block for part in pieces for block in part]
    return pl.pallas_call(
        functools.partial(join_body, devices, sizes),
        out_shape=jax.ShapeDtypeStruct((rows, devices * sum(sizes)), jnp.bfloat16),
        in_specs=[pl.BlockSpec(memory_space=pltpu.SMEM)] + in_vmem(len(flat)),
        out_specs=pl.BlockSpec(memory_space=pl.ANY),
        scratch_shapes=[pltpu.SemaphoreType.DMA((len(flat),))],
        compiler_params=pltpu.CompilerParams(vmem_limit_bytes=VMEM_LIMIT),
    )(me, *flat)


def body(query, key, value, valid_rows):
    devices = lax.axis_size("head")
    columns = lax.axis_size("tok")
    height = columns // TIME_TILES
    tiles, tokens, width = query.shape
    heads = width // HEAD_DIM // devices
    me = lax.axis_index("head").astype(jnp.int32).reshape(1)
    flat = [field.reshape(tiles * tokens, width) for field in (query, key, value)]
    own, sibling, own_query, far, far_query = pack(me, valid_rows, *flat, devices)
    rows = tiles * tokens

    sibling = swap_head(sibling, 1, devices)
    far = [swap_head(b, bit, devices) for bit, b in enumerate(far, 2)]
    far_query = [swap_head(b, bit, devices) for bit, b in enumerate(far_query, 2)]
    queries = [own_query, sibling[2 * rows :], *far_query]
    near = stack([own, sibling], [own.shape[0], 2 * rows])
    across = stack(far, [2 * rows] * len(far))
    slots = [(near, across)]
    if height > 1:
        slots += [
            tuple(swap_pairs(b, phase, 1, height, columns) for b in slots[0]) for phase in (0, 1)
        ]
    slots += [
        tuple(swap_pairs(b, phase, height, TIME_TILES, columns) for b in slot)
        for phase in (0, 1)
        for slot in slots
    ]
    near_rows = [0, own.shape[0]]
    far_rows = [2 * rows * i for i in range(devices - 2)]
    arrays = [across] + [mine for mine, _ in slots]
    groups = [(i, [(i, base) for base in near_rows]) for i in range(1, len(arrays))]
    groups[0][1].extend((0, base) for base in far_rows)
    state = attend(queries, arrays, groups, tiles, tokens, heads)

    arrays = [array for slot in slots[1:] for array in slot]
    groups = [(i, [(i + 1, base) for base in far_rows]) for i in range(0, len(arrays), 2)]
    cut = heads - heads // 3
    pieces = []
    for first, count in ((0, cut), (cut, heads - cut)):
        results = attend(
            queries, arrays, groups, tiles, tokens, count, first, state, weigh=int(first == 0)
        )
        results, state = lax.optimization_barrier((results, state))
        pieces.append(
            [results[0]] + [swap_head(b, bit, devices) for bit, b in enumerate(results[1:], 1)]
        )
    return join(me, pieces).reshape(tiles, tokens, width)


def solution(mesh):
    placed = (
        P(("clips", "tok"), "head", None),
        P(("clips", "tok"), "head", None),
        P(("clips", "tok"), "head", None),
        P(("clips", "tok")),
    )
    return jax.shard_map(
        body,
        mesh=mesh,
        in_specs=placed,
        out_specs=P(("clips", "tok"), "head", None),
        check_vma=False,
    )
```

```python
import functools
import math

import jax
import jax.numpy as jnp
from jax import lax
from jax.experimental import pallas as pl
from jax.experimental.pallas import tpu as pltpu
from jax.sharding import PartitionSpec as P

HEAD_DIM = 128
TILE_H = 8
TILE_W = 8
TIME_TILES = 4
COUNT_ROWS = 16
MASKED = -1e30
LARGEST_TOTAL = 2.0**100
SCALE = math.log2(math.e) / math.sqrt(HEAD_DIM)
VMEM_LIMIT = 24 * 2**20
WHOLE = False


def in_vmem(count):
    return [pl.BlockSpec(memory_space=pltpu.VMEM)] * count


def swap_head(block, bit, devices):
    return lax.ppermute(block, "head", [(i, i ^ bit) for i in range(devices)])


def swap_pairs(block, phase, stride, length, devices):
    route = []
    for i in range(devices):
        place = i // stride % length
        if place % 2 == phase and place + 1 < length:
            route += [(i, i + stride), (i + stride, i)]
    return lax.ppermute(block, "tok", route)


def pack_body(devices, part, counts_in, me_ref, q_ref, k_ref, v_ref, *rest):
    own_ref, sibling_ref, own_q_ref = rest[:3]
    far_refs, far_q_refs = rest[3 : 1 + devices], rest[1 + devices : -3]
    counts_ref, count_sem, sems = rest[-3:]
    rows = k_ref.shape[0]
    me = me_ref[0]

    def lanes(bit):
        return pl.ds(pl.multiple_of((me ^ bit) * part, HEAD_DIM), part)

    count_copy = pltpu.make_async_copy(counts_in, counts_ref, count_sem)
    count_copy.start()
    jobs = []
    targets = [(1, sibling_ref, 0)]
    targets += [(bit, far_refs[bit - 2], 0) for bit in range(2, devices)]
    for bit, ref, base in [*targets, (0, own_ref, 0)]:
        jobs += [
            (k_ref.at[:, lanes(bit)], ref.at[pl.ds(base, rows)]),
            (v_ref.at[:, lanes(bit)], ref.at[pl.ds(base + rows, rows)]),
        ]
    jobs += [
        (q_ref.at[:, lanes(1)], sibling_ref.at[pl.ds(2 * rows, rows)]),
        (q_ref.at[:, lanes(0)], own_q_ref),
    ]
    jobs += [
        (q_ref.at[:, lanes(bit)], far_q_refs[bit // 2 - 1].at[pl.ds(bit % 2 * rows, rows)])
        for bit in range(2, devices)
    ]
    copies = [pltpu.make_async_copy(src, dst, sems.at[i]) for i, (src, dst) in enumerate(jobs)]
    for copy in copies:
        copy.start()
    count_copy.wait()
    shape = (COUNT_ROWS, part)
    row = lax.broadcasted_iota(jnp.int32, shape, 0)
    filled = jnp.zeros(shape, jnp.float32)
    for tile in range(counts_ref.shape[0]):
        filled = jnp.where(row == tile, counts_ref[tile].astype(jnp.float32), filled)
    own_ref[pl.ds(2 * rows, COUNT_ROWS), :] = filled.astype(jnp.bfloat16)
    for copy in copies:
        copy.wait()


def pack(me, counts, query, key, value, devices):
    rows, width = query.shape
    part = width // devices
    far = devices - 2
    sizes = [2 * rows + COUNT_ROWS, 3 * rows, rows] + [2 * rows] * far + [2 * rows] * (far // 2)
    fields = [pltpu.with_memory_space_constraint(f, pltpu.HBM) for f in (query, key, value)]
    results = pl.pallas_call(
        functools.partial(pack_body, devices, part),
        out_shape=[pltpu.VMEM((size, part), jnp.bfloat16) for size in sizes],
        in_specs=[pl.BlockSpec(memory_space=pltpu.HBM), pl.BlockSpec(memory_space=pltpu.SMEM)]
        + [pl.BlockSpec(memory_space=pltpu.HBM)] * 3,
        out_specs=in_vmem(len(sizes)),
        scratch_shapes=[
            pltpu.SMEM(counts.shape, jnp.int32),
            pltpu.SemaphoreType.DMA,
            pltpu.SemaphoreType.DMA((3 * devices,)),
        ],
        compiler_params=pltpu.CompilerParams(vmem_limit_bytes=VMEM_LIMIT),
        cost_estimate=pl.CostEstimate(flops=0, bytes_accessed=12 * query.size, transcendentals=0),
    )(pltpu.with_memory_space_constraint(counts, pltpu.HBM), me, *fields)
    return results[0], results[1], results[2], results[3 : 3 + far], results[3 + far :]


def stack_body(jobs, *refs):
    blocks, out_ref, sems = refs[:-2], refs[-2], refs[-1]
    copies, base = [], 0
    for i, (size, lanes) in enumerate(jobs):
        source = blocks[i].at[pl.ds(0, size), lanes]
        copies.append(
            pltpu.make_async_copy(source, out_ref.at[pl.ds(base, size)], sems.at[i])
        )
        base += size
    for copy in copies:
        copy.start()
    for copy in copies:
        copy.wait()


def stack(blocks, sizes, start, width):
    jobs = [(size, pl.ds(start, width)) for size in sizes]
    return pl.pallas_call(
        functools.partial(stack_body, jobs),
        out_shape=pltpu.VMEM((sum(sizes), width), jnp.bfloat16),
        in_specs=in_vmem(len(blocks)),
        out_specs=pl.BlockSpec(memory_space=pltpu.VMEM),
        scratch_shapes=[pltpu.SemaphoreType.DMA((len(blocks),))],
        compiler_params=pltpu.CompilerParams(vmem_limit_bytes=VMEM_LIMIT),
        cost_estimate=pl.CostEstimate(
            flops=0, bytes_accessed=sum(sizes) * width, transcendentals=0
        ),
    )(*blocks)


def features(head):
    start = head * HEAD_DIM
    return pl.ds(start if isinstance(head, int) else pl.multiple_of(start, HEAD_DIM), HEAD_DIM)


def window_of(tile, tiles, groups):
    near = range(max(tile - 1, 0), min(tile + 2, tiles))
    return [(group, other) for other in near for group in range(len(groups))]


def gather(arrays, groups, window, start, tokens, lanes):
    return jnp.concatenate(
        [
            arrays[i][pl.ds(base + start + other * tokens, tokens), lanes]
            for group, other in window
            for i, base in groups[group][1]
        ],
        0,
    )


def counts_of(arrays, groups, rows):
    counts = [arrays[i][pl.ds(2 * rows, COUNT_ROWS), pl.ds(0, HEAD_DIM)] for i, _ in groups]
    return [count.astype(jnp.float32) for count in counts]


def bias_of(counts, groups, window, tokens):
    lane = lax.broadcasted_iota(jnp.int32, (1, HEAD_DIM), 1)
    row = (lane // TILE_W % TILE_H).astype(jnp.float32)
    parts = []
    for group, other in window:
        part = jnp.where(row < counts[group][other : other + 1], 0.0, MASKED)
        parts += [part] * (len(groups[group][1]) * tokens // HEAD_DIM)
    return jnp.concatenate(parts, 1)


def products(queries, keys):
    return lax.dot_general(
        queries, keys, (((1,), (1,)), ((), ())), preferred_element_type=jnp.float32
    )


def early_body(groups, operands, frames, tiles, tokens, heads, *refs):
    rows = tiles * tokens
    queries, arrays = refs[:frames], refs[frames : frames + operands]
    max_ref, total_ref, sum_ref = refs[frames + operands :]
    counts = counts_of(arrays, groups, rows)
    windows = [window_of(tile, tiles, groups) for tile in range(tiles)]
    biases = [bias_of(counts, groups, window, tokens) for window in windows]
    block = frames * tokens

    def scored(head, tile):
        lanes = features(head)
        asked = jnp.concatenate([ref[pl.ds(tile * tokens, tokens), lanes] for ref in queries], 0)
        scores = products(asked, gather(arrays, groups, windows[tile], 0, tokens, lanes))
        scores = scores + biases[tile]
        return scores, jnp.max(scores, axis=1, keepdims=True)

    steps = [(head, tile) for head in range(heads) for tile in range(tiles)]
    ahead = scored(*steps[0])
    for i, (head, tile) in enumerate(steps):
        scores, largest = ahead
        if i + 1 < len(steps):
            ahead = scored(*steps[i + 1])
        weight = jnp.exp2((scores - largest) * SCALE).astype(jnp.bfloat16)
        values = gather(arrays, groups, windows[tile], rows, tokens, features(head))
        values = jnp.concatenate([values, jnp.ones_like(values)], 1)
        summed = jnp.dot(weight, values, preferred_element_type=jnp.float32)
        place = pl.ds((head * tiles + tile) * block, block)
        max_ref[place, :] = jnp.broadcast_to(largest, (block, HEAD_DIM))
        sum_ref[place, :] = summed[:, :HEAD_DIM]
        total_ref[place, :] = summed[:, HEAD_DIM:]


def late_body(groups, operands, frames, tiles, tokens, heads, first, lane, *refs):
    rows = tiles * tokens
    queries, arrays = refs[:frames], refs[frames : frames + operands]
    max_ref, total_ref, sum_ref = refs[frames + operands : frames + operands + 3]
    outs = refs[frames + operands + 3 :]
    counts = counts_of(arrays, groups, rows)
    windows = [window_of(tile, tiles, groups) for tile in range(tiles)]
    block = frames * tokens

    def asked(head, tile):
        return jnp.concatenate(
            [ref[pl.ds(tile * tokens, tokens), features(first + head)] for ref in queries], 0
        )

    def place(head, tile):
        start = ((first + head) * tiles + tile) * block
        return pl.ds(start if isinstance(start, int) else pl.multiple_of(start, block), block)

    def write(head, tile, result):
        for frame in range(frames):
            outs[frame][pl.ds(tile * tokens, tokens), features(head)] = result[
                frame * tokens : (frame + 1) * tokens
            ]

    token = lax.broadcasted_iota(jnp.int32, (tokens, HEAD_DIM), 0)
    row = (token // TILE_W % TILE_H).astype(jnp.float32)
    real = [
        [jnp.where(row < count[n : n + 1], 1.0, 0.0).astype(jnp.bfloat16) for n in range(tiles)]
        for count in counts
    ]
    worst = jnp.zeros((block, HEAD_DIM), jnp.float32)
    for head in range(heads):
        lanes = features(lane + head)
        for tile, window in enumerate(windows):
            at = place(head, tile)
            scores = products(
                asked(head, tile), gather(arrays, groups, window, 0, tokens, lanes)
            )
            before = jnp.concatenate([max_ref[at, :]] * (scores.shape[1] // HEAD_DIM), 1)
            weight = jnp.exp2((scores - before) * SCALE).astype(jnp.bfloat16)
            kept = jnp.concatenate(
                [real[group][n] for group, n in window for _ in groups[group][1]], 0
            )
            values = gather(arrays, groups, window, rows, tokens, lanes) * kept
            summed = jnp.dot(
                weight,
                jnp.concatenate([values, kept], 1),
                preferred_element_type=jnp.float32,
            )
            total = total_ref[at, :] + summed[:, HEAD_DIM:]
            worst = jnp.where(total < LARGEST_TOTAL, worst, 1.0)
            result = (sum_ref[at, :] + summed[:, :HEAD_DIM]) / total
            write(head, tile, result.astype(jnp.bfloat16))

    @pl.when(jnp.max(worst) > 0.0)
    def _():
        def one_head(head, _):
            lanes = features(lane + head)
            for tile, window in enumerate(windows):
                at = place(head, tile)
                scores = products(
                    asked(head, tile), gather(arrays, groups, window, 0, tokens, lanes)
                )
                scores = scores + bias_of(counts, groups, window, tokens)
                before = max_ref[at, :]
                largest = jnp.maximum(before[:, :1], jnp.max(scores, axis=1, keepdims=True))
                shrink = jnp.exp2((before - largest) * SCALE)
                weight = jnp.exp2((scores - largest) * SCALE)
                total = jnp.sum(weight, axis=1, keepdims=True) + total_ref[at, :] * shrink
                summed = jnp.dot(
                    weight.astype(jnp.bfloat16),
                    gather(arrays, groups, window, rows, tokens, lanes),
                    preferred_element_type=jnp.float32,
                )
                result = (summed + sum_ref[at, :] * shrink) / total
                write(head, tile, result.astype(jnp.bfloat16))
            return 0

        lax.fori_loop(0, heads, one_head, 0)


def attend(queries, arrays, groups, tiles, tokens, heads, first=0, base=0, state=(), weigh=1):
    frames = len(queries)
    operands = [*queries, *arrays, *state]
    size = sum(len(fields) for _, fields in groups)
    pairs = heads * (3 * tiles - 2) * size * tokens * frames * tokens
    shape = (groups, len(arrays), frames, tiles, tokens, heads)
    if state:
        outs = [pltpu.VMEM((tiles * tokens, heads * HEAD_DIM), jnp.bfloat16)] * frames
        kernel = functools.partial(late_body, *shape, first, base)
    else:
        outs = [pltpu.VMEM((heads * tiles * frames * tokens, HEAD_DIM), jnp.float32)] * 3
        kernel = functools.partial(early_body, *shape)
    return pl.pallas_call(
        kernel,
        out_shape=outs,
        in_specs=in_vmem(len(operands)),
        out_specs=in_vmem(len(outs)),
        compiler_params=pltpu.CompilerParams(vmem_limit_bytes=VMEM_LIMIT),
        cost_estimate=pl.CostEstimate(
            flops=weigh * 4 * HEAD_DIM * pairs, bytes_accessed=0, transcendentals=weigh * pairs
        ),
    )(*operands)


def join_body(jobs, part, me_ref, *rest):
    out_ref, sems = rest[-2:]
    me = me_ref[0]
    copies = []
    for i, (bit, base) in enumerate(jobs):
        lanes = pl.ds(pl.multiple_of((me ^ bit) * part + base, HEAD_DIM), rest[i].shape[1])
        copies.append(pltpu.make_async_copy(rest[i], out_ref.at[:, lanes], sems.at[i]))
    for copy in copies:
        copy.start()
    for copy in copies:
        copy.wait()


def join(me, pieces, rows, part, devices):
    jobs = [piece[:2] for piece in pieces]
    return pl.pallas_call(
        functools.partial(join_body, jobs, part),
        out_shape=jax.ShapeDtypeStruct((rows, devices * part), jnp.bfloat16),
        in_specs=[pl.BlockSpec(memory_space=pltpu.SMEM)] + in_vmem(len(pieces)),
        out_specs=pl.BlockSpec(memory_space=pl.ANY),
        scratch_shapes=[pltpu.SemaphoreType.DMA((len(pieces),))],
        compiler_params=pltpu.CompilerParams(vmem_limit_bytes=VMEM_LIMIT),
    )(me, *(piece[2] for piece in pieces))


def body(query, key, value, valid_rows):
    devices = lax.axis_size("head")
    columns = lax.axis_size("tok")
    height = columns // TIME_TILES
    tiles, tokens, width = query.shape
    heads = width // HEAD_DIM // devices
    me = lax.axis_index("head").astype(jnp.int32).reshape(1)
    flat = [field.reshape(tiles * tokens, width) for field in (query, key, value)]
    own, sibling, own_query, far, far_query = pack(me, valid_rows, *flat, devices)
    rows = tiles * tokens

    part = heads * HEAD_DIM

    def by_height(block):
        if height == 1:
            return [block]
        return [block] + [swap_pairs(block, phase, 1, height, columns) for phase in (0, 1)]

    def by_time(blocks):
        return [
            swap_pairs(b, phase, height, TIME_TILES, columns) for phase in (0, 1) for b in blocks
        ]

    sibling = swap_head(sibling, 1, devices)
    far = [swap_head(b, bit, devices) for bit, b in enumerate(far, 2)]
    far_query = [swap_head(b, 2 * i + 2, devices) for i, b in enumerate(far_query)]
    near = by_height(stack([own, sibling], [own.shape[0], 2 * rows], 0, part))
    near = near + by_time(near)

    queries = [own_query, sibling[2 * rows :]]
    for block in far_query:
        queries += [block[:rows], swap_head(block[rows:], 1, devices)]

    cut = heads - heads // 3
    parts = [(0, heads)] if WHOLE else [(0, cut), (cut, heads - cut)]
    across = []
    for first, count in parts:
        block = stack(far, [2 * rows] * len(far), first * HEAD_DIM, count * HEAD_DIM)
        if first:
            block, *near = lax.optimization_barrier((block, *near))
        block = by_height(block)
        across.append(block[1:] + by_time(block))
    parts = [(0, cut), (cut, heads - cut)]

    near_rows = [0, own.shape[0]]
    far_rows = [2 * rows * i for i in range(devices - 2)]
    arrays = near + far
    groups = [(i, [(i, base) for base in near_rows]) for i in range(len(near))]
    groups[0][1].extend((len(near) + i, 0) for i in range(len(far)))
    state = attend(queries, arrays, groups, tiles, tokens, heads)

    pieces = []
    for i, (first, count) in enumerate(parts):
        others = across[min(i, len(across) - 1)]
        groups = [
            (i, [(len(others) + i, base) for base in far_rows]) for i in range(len(others))
        ]
        base = first if WHOLE else 0
        results = attend(
            queries, near[1:] + others, groups, tiles, tokens, count, first, base, state
        )
        results = list(results)
        results[1] = swap_head(results[1], 1, devices)
        if i == 0:
            *state, results[1] = lax.optimization_barrier((*state, results[1]))
        pieces += [
            (bit, first * HEAD_DIM, swap_head(b, bit, devices) if bit > 1 else b)
            for bit, b in enumerate(results)
        ]
    return join(me, pieces, rows, part, devices).reshape(tiles, tokens, width)


def solution(mesh):
    placed = (
        P(("clips", "tok"), "head", None),
        P(("clips", "tok"), "head", None),
        P(("clips", "tok"), "head", None),
        P(("clips", "tok")),
    )
    return jax.shard_map(
        body,
        mesh=mesh,
        in_specs=placed,
        out_specs=P(("clips", "tok"), "head", None),
        check_vma=False,
    )
```

```python
import functools
import math

import jax
import jax.numpy as jnp
from jax import lax
from jax.experimental import pallas as pl
from jax.experimental.pallas import tpu as pltpu
from jax.sharding import PartitionSpec as P

HEAD_DIM = 128
TILE_H = 8
TILE_W = 8
TIME_TILES = 4
COUNT_ROWS = 16
MASKED = -1e30
LARGEST_TOTAL = 2.0**100
SCALE = math.log2(math.e) / math.sqrt(HEAD_DIM)
VMEM_LIMIT = 24 * 2**20
WHOLE = False


def in_vmem(count):
    return [pl.BlockSpec(memory_space=pltpu.VMEM)] * count


def swap_head(block, bit, devices):
    return lax.ppermute(block, "head", [(i, i ^ bit) for i in range(devices)])


def swap_pairs(block, phase, stride, length, devices):
    route = []
    for i in range(devices):
        place = i // stride % length
        if place % 2 == phase and place + 1 < length:
            route += [(i, i + stride), (i + stride, i)]
    return lax.ppermute(block, "tok", route)


def pack_body(devices, part, counts_in, me_ref, q_ref, k_ref, v_ref, *rest):
    own_ref, sibling_ref, own_q_ref = rest[:3]
    far_refs, far_q_refs = rest[3 : 1 + devices], rest[1 + devices : -3]
    counts_ref, count_sem, sems = rest[-3:]
    rows = k_ref.shape[0]
    me = me_ref[0]

    def lanes(bit):
        return pl.ds(pl.multiple_of((me ^ bit) * part, HEAD_DIM), part)

    count_copy = pltpu.make_async_copy(counts_in, counts_ref, count_sem)
    count_copy.start()
    jobs = []
    targets = [(1, sibling_ref, 0)]
    targets += [(bit, far_refs[bit - 2], 0) for bit in range(2, devices)]
    for bit, ref, base in [*targets, (0, own_ref, 0)]:
        jobs += [
            (k_ref.at[:, lanes(bit)], ref.at[pl.ds(base, rows)]),
            (v_ref.at[:, lanes(bit)], ref.at[pl.ds(base + rows, rows)]),
        ]
    jobs += [
        (q_ref.at[:, lanes(1)], sibling_ref.at[pl.ds(2 * rows, rows)]),
        (q_ref.at[:, lanes(0)], own_q_ref),
    ]
    for i, ref in enumerate(far_q_refs):
        passed = sibling_ref.at[pl.ds((3 + i) * rows, rows)]
        jobs += [(q_ref.at[:, lanes(2 * i + 2)], ref), (q_ref.at[:, lanes(2 * i + 3)], passed)]
    copies = [pltpu.make_async_copy(src, dst, sems.at[i]) for i, (src, dst) in enumerate(jobs)]
    for copy in copies:
        copy.start()
    count_copy.wait()
    shape = (COUNT_ROWS, part)
    row = lax.broadcasted_iota(jnp.int32, shape, 0)
    filled = jnp.zeros(shape, jnp.float32)
    for tile in range(counts_ref.shape[0]):
        filled = jnp.where(row == tile, counts_ref[tile].astype(jnp.float32), filled)
    own_ref[pl.ds(2 * rows, COUNT_ROWS), :] = filled.astype(jnp.bfloat16)
    for copy in copies:
        copy.wait()


def pack(me, counts, query, key, value, devices):
    rows, width = query.shape
    part = width // devices
    far = devices - 2
    sizes = [2 * rows + COUNT_ROWS, (3 + far // 2) * rows, rows]
    sizes += [2 * rows] * far + [rows] * (far // 2)
    fields = [pltpu.with_memory_space_constraint(f, pltpu.HBM) for f in (query, key, value)]
    results = pl.pallas_call(
        functools.partial(pack_body, devices, part),
        out_shape=[pltpu.VMEM((size, part), jnp.bfloat16) for size in sizes],
        in_specs=[pl.BlockSpec(memory_space=pltpu.HBM), pl.BlockSpec(memory_space=pltpu.SMEM)]
        + [pl.BlockSpec(memory_space=pltpu.HBM)] * 3,
        out_specs=in_vmem(len(sizes)),
        scratch_shapes=[
            pltpu.SMEM(counts.shape, jnp.int32),
            pltpu.SemaphoreType.DMA,
            pltpu.SemaphoreType.DMA((3 * devices,)),
        ],
        compiler_params=pltpu.CompilerParams(vmem_limit_bytes=VMEM_LIMIT),
        cost_estimate=pl.CostEstimate(flops=0, bytes_accessed=12 * query.size, transcendentals=0),
    )(pltpu.with_memory_space_constraint(counts, pltpu.HBM), me, *fields)
    return results[0], results[1], results[2], results[3 : 3 + far], results[3 + far :]


def stack_body(jobs, *refs):
    blocks, out_ref, sems = refs[:-2], refs[-2], refs[-1]
    copies, base = [], 0
    for i, (first, size, lanes) in enumerate(jobs):
        source = blocks[i].at[pl.ds(first, size), lanes]
        copies.append(
            pltpu.make_async_copy(source, out_ref.at[pl.ds(base, size)], sems.at[i])
        )
        base += size
    for copy in copies:
        copy.start()
    for copy in copies:
        copy.wait()


def stack(blocks, spans, start, width, flops=0, pad=0):
    jobs = [(first, size, pl.ds(start, width)) for first, size in spans]
    rows = sum(size for _, size in spans)
    return pl.pallas_call(
        functools.partial(stack_body, jobs),
        out_shape=pltpu.VMEM((rows + pad, width), jnp.bfloat16),
        in_specs=in_vmem(len(blocks)),
        out_specs=pl.BlockSpec(memory_space=pltpu.VMEM),
        scratch_shapes=[pltpu.SemaphoreType.DMA((len(blocks),))],
        compiler_params=pltpu.CompilerParams(vmem_limit_bytes=VMEM_LIMIT),
        cost_estimate=pl.CostEstimate(
            flops=flops, bytes_accessed=rows * width, transcendentals=0
        ),
    )(*blocks)


def features(head):
    start = head * HEAD_DIM
    return pl.ds(start if isinstance(head, int) else pl.multiple_of(start, HEAD_DIM), HEAD_DIM)


def window_of(tile, tiles, groups):
    near = range(max(tile - 1, 0), min(tile + 2, tiles))
    return [(group, other) for other in near for group in range(len(groups))]


def gather(arrays, groups, window, start, tokens, lanes):
    return jnp.concatenate(
        [
            arrays[i][pl.ds(base + start + other * tokens, tokens), lanes]
            for group, other in window
            for i, base in groups[group][1]
        ],
        0,
    )


def counts_of(arrays, groups, rows):
    counts = [arrays[i][pl.ds(2 * rows, COUNT_ROWS), pl.ds(0, HEAD_DIM)] for i, _ in groups]
    return [count.astype(jnp.float32) for count in counts]


def bias_of(counts, groups, window, tokens):
    lane = lax.broadcasted_iota(jnp.int32, (1, HEAD_DIM), 1)
    row = (lane // TILE_W % TILE_H).astype(jnp.float32)
    parts = []
    for group, other in window:
        part = jnp.where(row < counts[group][other : other + 1], 0.0, MASKED)
        parts += [part] * (len(groups[group][1]) * tokens // HEAD_DIM)
    return jnp.concatenate(parts, 1)


def products(queries, keys):
    return lax.dot_general(
        queries, keys, (((1,), (1,)), ((), ())), preferred_element_type=jnp.float32
    )


def early_body(groups, operands, frames, tiles, tokens, heads, *refs):
    rows = tiles * tokens
    queries, arrays = refs[:frames], refs[frames : frames + operands]
    max_ref, total_ref, sum_ref = refs[frames + operands :]
    counts = counts_of(arrays, groups, rows)
    windows = [window_of(tile, tiles, groups) for tile in range(tiles)]
    biases = [bias_of(counts, groups, window, tokens) for window in windows]
    block = frames * tokens

    def scored(head, tile):
        lanes = features(head)
        asked = jnp.concatenate([ref[pl.ds(tile * tokens, tokens), lanes] for ref in queries], 0)
        scores = products(asked, gather(arrays, groups, windows[tile], 0, tokens, lanes))
        scores = scores + biases[tile]
        return scores, jnp.max(scores, axis=1, keepdims=True)

    steps = [(head, tile) for head in range(heads) for tile in range(tiles)]
    ahead = scored(*steps[0])
    for i, (head, tile) in enumerate(steps):
        scores, largest = ahead
        if i + 1 < len(steps):
            ahead = scored(*steps[i + 1])
        weight = jnp.exp2((scores - largest) * SCALE).astype(jnp.bfloat16)
        values = gather(arrays, groups, windows[tile], rows, tokens, features(head))
        values = jnp.concatenate([values, jnp.ones_like(values)], 1)
        summed = jnp.dot(weight, values, preferred_element_type=jnp.float32)
        place = pl.ds((head * tiles + tile) * block, block)
        max_ref[place, :] = jnp.broadcast_to(largest, (block, HEAD_DIM))
        sum_ref[place, :] = summed[:, :HEAD_DIM]
        total_ref[place, :] = summed[:, HEAD_DIM:]


def late_body(groups, operands, frames, tiles, tokens, heads, states, first, lane, *refs):
    rows = tiles * tokens
    queries, arrays = refs[:frames], refs[frames : frames + operands]
    left = refs[frames + operands : frames + operands + 3 * states]
    outs = refs[frames + operands + 3 * states :]
    counts = counts_of(arrays, groups, rows)
    windows = [window_of(tile, tiles, groups) for tile in range(tiles)]
    block = frames * tokens
    share = block // states

    def asked(head, tile):
        return jnp.concatenate(
            [ref[pl.ds(tile * tokens, tokens), features(first + head)] for ref in queries], 0
        )

    def early(head, tile):
        start = ((first + head) * tiles + tile) * share
        at = pl.ds(start if isinstance(start, int) else pl.multiple_of(start, share), share)
        return [jnp.concatenate([ref[at, :] for ref in left[which::3]], 0) for which in range(3)]

    def write(head, tile, result):
        for frame in range(frames):
            outs[frame][pl.ds(tile * tokens, tokens), features(head)] = result[
                frame * tokens : (frame + 1) * tokens
            ]

    token = lax.broadcasted_iota(jnp.int32, (tokens, HEAD_DIM), 0)
    row = (token // TILE_W % TILE_H).astype(jnp.float32)
    real = [
        [jnp.where(row < count[n : n + 1], 1.0, 0.0).astype(jnp.bfloat16) for n in range(tiles)]
        for count in counts
    ]
    worst = jnp.zeros((block, HEAD_DIM), jnp.float32)
    for head in range(heads):
        lanes = features(lane + head)
        for tile, window in enumerate(windows):
            largest, total, summed = early(head, tile)
            scores = products(
                asked(head, tile), gather(arrays, groups, window, 0, tokens, lanes)
            )
            largest = jnp.concatenate([largest] * (scores.shape[1] // HEAD_DIM), 1)
            weight = jnp.exp2((scores - largest) * SCALE).astype(jnp.bfloat16)
            kept = jnp.concatenate(
                [real[group][n] for group, n in window for _ in groups[group][1]], 0
            )
            values = gather(arrays, groups, window, rows, tokens, lanes) * kept
            added = jnp.dot(
                weight,
                jnp.concatenate([values, kept], 1),
                preferred_element_type=jnp.float32,
            )
            total = total + added[:, HEAD_DIM:]
            worst = jnp.where(total < LARGEST_TOTAL, worst, 1.0)
            result = (summed + added[:, :HEAD_DIM]) / total
            write(head, tile, result.astype(jnp.bfloat16))

    @pl.when(jnp.max(worst) > 0.0)
    def _():
        def one_head(head, _):
            lanes = features(lane + head)
            for tile, window in enumerate(windows):
                before, total, summed = early(head, tile)
                scores = products(
                    asked(head, tile), gather(arrays, groups, window, 0, tokens, lanes)
                )
                scores = scores + bias_of(counts, groups, window, tokens)
                largest = jnp.maximum(before[:, :1], jnp.max(scores, axis=1, keepdims=True))
                shrink = jnp.exp2((before - largest) * SCALE)
                weight = jnp.exp2((scores - largest) * SCALE)
                total = jnp.sum(weight, axis=1, keepdims=True) + total * shrink
                added = jnp.dot(
                    weight.astype(jnp.bfloat16),
                    gather(arrays, groups, window, rows, tokens, lanes),
                    preferred_element_type=jnp.float32,
                )
                result = (added + summed * shrink) / total
                write(head, tile, result.astype(jnp.bfloat16))
            return 0

        lax.fori_loop(0, heads, one_head, 0)


def attend(queries, arrays, groups, tiles, tokens, heads, first=0, base=0, state=(), weigh=0):
    weigh = 0 if state else 0
    frames = len(queries)
    operands = [*queries, *arrays, *state]
    size = sum(len(fields) for _, fields in groups)
    pairs = heads * (3 * tiles - 2) * size * tokens * frames * tokens
    shape = (groups, len(arrays), frames, tiles, tokens, heads)
    if state:
        outs = [pltpu.VMEM((tiles * tokens, heads * HEAD_DIM), jnp.bfloat16)] * frames
        kernel = functools.partial(late_body, *shape, len(state) // 3, first, base)
    else:
        outs = [pltpu.VMEM((heads * tiles * frames * tokens, HEAD_DIM), jnp.float32)] * 3
        kernel = functools.partial(early_body, *shape)
    return pl.pallas_call(
        kernel,
        out_shape=outs,
        in_specs=in_vmem(len(operands)),
        out_specs=in_vmem(len(outs)),
        compiler_params=pltpu.CompilerParams(vmem_limit_bytes=VMEM_LIMIT),
        cost_estimate=pl.CostEstimate(
            flops=weigh * 4 * HEAD_DIM * pairs, bytes_accessed=0, transcendentals=weigh * pairs
        ),
    )(*operands)


def join_body(jobs, part, me_ref, *rest):
    out_ref, sems = rest[-2:]
    me = me_ref[0]
    copies = []
    for i, (bit, base) in enumerate(jobs):
        lanes = pl.ds(pl.multiple_of((me ^ bit) * part + base, HEAD_DIM), rest[i].shape[1])
        copies.append(pltpu.make_async_copy(rest[i], out_ref.at[:, lanes], sems.at[i]))
    for copy in copies:
        copy.start()
    for copy in copies:
        copy.wait()


def join(me, pieces, rows, part, devices):
    jobs = [piece[:2] for piece in pieces]
    return pl.pallas_call(
        functools.partial(join_body, jobs, part),
        out_shape=jax.ShapeDtypeStruct((rows, devices * part), jnp.bfloat16),
        in_specs=[pl.BlockSpec(memory_space=pltpu.SMEM)] + in_vmem(len(pieces)),
        out_specs=pl.BlockSpec(memory_space=pl.ANY),
        scratch_shapes=[pltpu.SemaphoreType.DMA((len(pieces),))],
        compiler_params=pltpu.CompilerParams(vmem_limit_bytes=VMEM_LIMIT),
    )(me, *(piece[2] for piece in pieces))


def body(query, key, value, valid_rows):
    devices = lax.axis_size("head")
    columns = lax.axis_size("tok")
    height = columns // TIME_TILES
    tiles, tokens, width = query.shape
    heads = width // HEAD_DIM // devices
    me = lax.axis_index("head").astype(jnp.int32).reshape(1)
    flat = [field.reshape(tiles * tokens, width) for field in (query, key, value)]
    own, sibling, own_query, far, far_query = pack(me, valid_rows, *flat, devices)
    rows = tiles * tokens

    part = heads * HEAD_DIM

    def by_height(block):
        if height == 1:
            return [block]
        return [block] + [swap_pairs(block, phase, 1, height, columns) for phase in (0, 1)]

    def by_time(blocks):
        return [
            swap_pairs(b, phase, height, TIME_TILES, columns) for phase in (0, 1) for b in blocks
        ]

    sibling = swap_head(sibling, 1, devices)
    far = [swap_head(b, bit, devices) for bit, b in enumerate(far, 2)]
    far_query = [
        swap_head(
            stack([b, sibling], [(0, rows), ((3 + i) * rows, rows)], 0, part, 0, 0), 2 * i + 2, devices
        )
        for i, b in enumerate(far_query)
    ]
    near = by_height(stack([own, sibling], [(0, own.shape[0]), (0, 2 * rows)], 0, part))
    near = near + by_time(near)

    queries = [own_query, sibling[2 * rows : 3 * rows]]
    for block in far_query:
        queries += [block[:rows], block[rows : 2 * rows]]

    cut = heads - heads // 3
    parts = [(0, heads)] if WHOLE else [(0, cut), (cut, heads - cut)]
    across = []
    for first, count in parts:
        block = stack(
            far,
            [(0, 2 * rows)] * len(far),
            first * HEAD_DIM,
            count * HEAD_DIM,
            0 if first else 2000000000,
            0 if first else 0,
        )
        if first:
            block, *near = lax.optimization_barrier((block, *near))
        block = by_height(block)
        across.append(block[1:] + by_time(block))
    parts = [(0, cut), (cut, heads - cut)]

    near_rows = [0, own.shape[0]]
    far_rows = [2 * rows * i for i in range(devices - 2)]
    arrays = near + far
    groups = [(i, [(i, base) for base in near_rows]) for i in range(len(near))]
    groups[0][1].extend((len(near) + i, 0) for i in range(len(far)))
    state = [
        left
        for part in (queries,)
        for left in attend(part, arrays, groups, tiles, tokens, heads)
    ]

    pieces = []
    for i, (first, count) in enumerate(parts):
        others = across[min(i, len(across) - 1)]
        groups = [
            (i, [(len(others) + i, base) for base in far_rows]) for i in range(len(others))
        ]
        base = first if WHOLE else 0
        results = attend(
            queries, near[1:] + others, groups, tiles, tokens, count, first, base, state
        )
        results = list(results)
        results[1] = swap_head(results[1], 1, devices)
        if i == 0:
            *state, results[1] = lax.optimization_barrier((*state, results[1]))
        pieces += [
            (bit, first * HEAD_DIM, swap_head(b, bit, devices) if bit > 1 else b)
            for bit, b in enumerate(results)
        ]
    return join(me, pieces, rows, part, devices).reshape(tiles, tokens, width)


def solution(mesh):
    placed = (
        P(("clips", "tok"), "head", None),
        P(("clips", "tok"), "head", None),
        P(("clips", "tok"), "head", None),
        P(("clips", "tok")),
    )
    return jax.shard_map(
        body,
        mesh=mesh,
        in_specs=placed,
        out_specs=P(("clips", "tok"), "head", None),
        check_vma=False,
    )
```

```python
import functools
import math

import jax
import jax.numpy as jnp
from jax import lax
from jax.experimental import pallas as pl
from jax.experimental.pallas import tpu as pltpu
from jax.sharding import PartitionSpec as P

HEAD_DIM = 128
TILE_H = 8
TILE_W = 8
TIME_TILES = 4
COUNT_ROWS = 16
MASKED = -1e30
LARGEST_TOTAL = 2.0**100
SCALE = math.log2(math.e) / math.sqrt(HEAD_DIM)
VMEM_LIMIT = 24 * 2**20
FIRST_FLOPS = 2500000000
EARLY_FLOPS = 0


def in_vmem(count):
    return [pl.BlockSpec(memory_space=pltpu.VMEM)] * count


def swap_head(block, bit, devices):
    return lax.ppermute(block, "head", [(i, i ^ bit) for i in range(devices)])


def swap_pairs(block, phase, stride, length, devices):
    route = []
    for i in range(devices):
        place = i // stride % length
        if place % 2 == phase and place + 1 < length:
            route += [(i, i + stride), (i + stride, i)]
    return lax.ppermute(block, "tok", route)


def pack_body(devices, heads, counts_in, me_ref, q_ref, k_ref, v_ref, *rest):
    far = devices - 2
    own_ref, sibling_ref, passed_ref, own_q_ref = rest[:4]
    far_refs, last_refs = rest[4 : 4 + far], rest[4 + far : -3]
    counts_ref, count_sem, sems = rest[-3:]
    rows = k_ref.shape[0]
    me = me_ref[0]

    def lanes(bit, first=0, count=heads):
        start = ((me ^ bit) * heads + first) * HEAD_DIM
        return pl.ds(pl.multiple_of(start, HEAD_DIM), count * HEAD_DIM)

    count_copy = pltpu.make_async_copy(counts_in, counts_ref, count_sem)
    count_copy.start()
    jobs = [
        (k_ref.at[:, lanes(1)], sibling_ref.at[pl.ds(0, rows)]),
        (v_ref.at[:, lanes(1)], sibling_ref.at[pl.ds(rows, rows)]),
        (q_ref.at[:, lanes(1)], sibling_ref.at[pl.ds(2 * rows, rows)]),
    ]
    for bit, ref in enumerate(far_refs, 2):
        jobs += [
            (k_ref.at[:, lanes(bit, 0, heads - 1)], ref.at[pl.ds(0, rows)]),
            (v_ref.at[:, lanes(bit, 0, heads - 1)], ref.at[pl.ds(rows, rows)]),
        ]
    jobs += [
        (k_ref.at[:, lanes(0)], own_ref.at[pl.ds(0, rows)]),
        (v_ref.at[:, lanes(0)], own_ref.at[pl.ds(rows, rows)]),
        (q_ref.at[:, lanes(0)], own_q_ref),
    ]
    for bit in range(2, devices):
        pair = bit // 2 - 1
        ref, base = (passed_ref, pair * (heads + 2)) if bit % 2 else (last_refs[pair], 0)
        sources = [q_ref.at[:, lanes(bit, head, 1)] for head in range(heads)]
        sources += [k_ref.at[:, lanes(bit, heads - 1, 1)], v_ref.at[:, lanes(bit, heads - 1, 1)]]
        jobs += [
            (source, ref.at[pl.ds((base + i) * rows, rows)]) for i, source in enumerate(sources)
        ]
    copies = [pltpu.make_async_copy(src, dst, sems.at[i]) for i, (src, dst) in enumerate(jobs)]
    for copy in copies:
        copy.start()
    count_copy.wait()
    shape = (COUNT_ROWS, own_ref.shape[1])
    row = lax.broadcasted_iota(jnp.int32, shape, 0)
    filled = jnp.zeros(shape, jnp.float32)
    for tile in range(counts_ref.shape[0]):
        filled = jnp.where(row == tile, counts_ref[tile].astype(jnp.float32), filled)
    own_ref[pl.ds(2 * rows, COUNT_ROWS), :] = filled.astype(jnp.bfloat16)
    for copy in copies:
        copy.wait()


def pack(me, counts, query, key, value, devices):
    rows, width = query.shape
    part = width // devices
    heads = part // HEAD_DIM
    far = devices - 2
    shapes = [(2 * rows + COUNT_ROWS, part), (3 * rows, part)]
    shapes += [(far // 2 * (heads + 2) * rows, HEAD_DIM), (rows, part)]
    shapes += [(2 * rows, part - HEAD_DIM)] * far + [((heads + 2) * rows, HEAD_DIM)] * (far // 2)
    fields = [pltpu.with_memory_space_constraint(f, pltpu.HBM) for f in (query, key, value)]
    results = pl.pallas_call(
        functools.partial(pack_body, devices, heads),
        out_shape=[pltpu.VMEM(shape, jnp.bfloat16) for shape in shapes],
        in_specs=[pl.BlockSpec(memory_space=pltpu.HBM), pl.BlockSpec(memory_space=pltpu.SMEM)]
        + [pl.BlockSpec(memory_space=pltpu.HBM)] * 3,
        out_specs=in_vmem(len(shapes)),
        scratch_shapes=[
            pltpu.SMEM(counts.shape, jnp.int32),
            pltpu.SemaphoreType.DMA,
            pltpu.SemaphoreType.DMA((6 + far * (heads + 4),)),
        ],
        compiler_params=pltpu.CompilerParams(vmem_limit_bytes=VMEM_LIMIT),
        cost_estimate=pl.CostEstimate(flops=0, bytes_accessed=12 * query.size, transcendentals=0),
    )(pltpu.with_memory_space_constraint(counts, pltpu.HBM), me, *fields)
    return (*results[:4], results[4 : 4 + far], results[4 + far :])


def stack_body(jobs, after, *refs):
    blocks, out_ref, sems = refs[: -2 - after], refs[-2], refs[-1]
    copies, base = [], 0
    for i, (first, size) in enumerate(jobs):
        source = blocks[i].at[pl.ds(first, size)]
        copies.append(
            pltpu.make_async_copy(source, out_ref.at[pl.ds(base, size)], sems.at[i])
        )
        base += size
    for copy in copies:
        copy.start()
    for copy in copies:
        copy.wait()


def stack(blocks, spans, flops=0, after=()):
    width = blocks[0].shape[1]
    rows = sum(size for _, size in spans)
    return pl.pallas_call(
        functools.partial(stack_body, spans, len(after)),
        out_shape=pltpu.VMEM((rows, width), jnp.bfloat16),
        in_specs=in_vmem(len(blocks) + len(after)),
        out_specs=pl.BlockSpec(memory_space=pltpu.VMEM),
        scratch_shapes=[pltpu.SemaphoreType.DMA((len(blocks),))],
        compiler_params=pltpu.CompilerParams(vmem_limit_bytes=VMEM_LIMIT),
        cost_estimate=pl.CostEstimate(
            flops=flops, bytes_accessed=rows * width, transcendentals=0
        ),
    )(*blocks, *after)


def features(head):
    return pl.ds(aligned(head * HEAD_DIM, HEAD_DIM), HEAD_DIM)


def window_of(tile, tiles, groups):
    near = range(max(tile - 1, 0), min(tile + 2, tiles))
    return [(group, other) for other in near for group in range(len(groups))]


def aligned(start, unit):
    return start if isinstance(start, int) else pl.multiple_of(start, unit)


def gather(arrays, groups, window, start, tokens, head):
    blocks = []
    for group, other in window:
        for field in groups[group][1]:
            index, base, first = field[0]
            for segment in field[1:]:
                if head >= segment[2]:
                    index, base, first = segment
            rows = pl.ds(base + start + other * tokens, tokens)
            blocks.append(arrays[index][rows, features(head - first)])
    return jnp.concatenate(blocks, 0)


def asked_of(queries, layout, head, tile, tokens, rows):
    blocks = []
    for index, base, by_rows in layout:
        if by_rows:
            at = pl.ds(aligned(base + head * rows + tile * tokens, tokens), tokens)
            blocks.append(queries[index][at, :])
        else:
            blocks.append(queries[index][pl.ds(base + tile * tokens, tokens), features(head)])
    return jnp.concatenate(blocks, 0)


def counts_of(arrays, groups, rows):
    counts = [arrays[i][pl.ds(2 * rows, COUNT_ROWS), pl.ds(0, HEAD_DIM)] for i, _ in groups]
    return [count.astype(jnp.float32) for count in counts]


def bias_of(counts, groups, window, tokens):
    lane = lax.broadcasted_iota(jnp.int32, (1, HEAD_DIM), 1)
    row = (lane // TILE_W % TILE_H).astype(jnp.float32)
    parts = []
    for group, other in window:
        part = jnp.where(row < counts[group][other : other + 1], 0.0, MASKED)
        parts += [part] * (len(groups[group][1]) * tokens // HEAD_DIM)
    return jnp.concatenate(parts, 1)


def products(queries, keys):
    return lax.dot_general(
        queries, keys, (((1,), (1,)), ((), ())), preferred_element_type=jnp.float32
    )


def early_body(groups, operands, jobs, asked, tiles, tokens, *refs):
    rows = tiles * tokens
    queries, arrays = refs[:asked], refs[asked : asked + operands]
    outs = refs[asked + operands :]
    counts = counts_of(arrays, groups, rows)
    windows = [window_of(tile, tiles, groups) for tile in range(tiles)]
    biases = [bias_of(counts, groups, window, tokens) for window in windows]

    def scored(job, head, tile):
        scores = products(
            asked_of(queries, jobs[job][0], head, tile, tokens, rows),
            gather(arrays, groups, windows[tile], 0, tokens, head),
        )
        scores = scores + biases[tile]
        return scores, jnp.max(scores, axis=1, keepdims=True)

    steps = [
        (job, head, tile)
        for job, (_, heads) in enumerate(jobs)
        for head in heads
        for tile in range(tiles)
    ]
    ahead = scored(*steps[0])
    for i, (job, head, tile) in enumerate(steps):
        scores, largest = ahead
        if i + 1 < len(steps):
            ahead = scored(*steps[i + 1])
        weight = jnp.exp2((scores - largest) * SCALE).astype(jnp.bfloat16)
        values = gather(arrays, groups, windows[tile], rows, tokens, head)
        values = jnp.concatenate([values, jnp.ones_like(values)], 1)
        summed = jnp.dot(weight, values, preferred_element_type=jnp.float32)
        layout, heads = jobs[job]
        block = len(layout) * tokens
        place = pl.ds(((head - heads[0]) * tiles + tile) * block, block)
        max_ref, total_ref, sum_ref = outs[3 * job : 3 * job + 3]
        max_ref[place, :] = jnp.broadcast_to(largest, (block, HEAD_DIM))
        sum_ref[place, :] = summed[:, :HEAD_DIM]
        total_ref[place, :] = summed[:, HEAD_DIM:]


def late_body(groups, operands, layout, asked, tiles, tokens, heads, first, parts, *refs):
    rows = tiles * tokens
    queries, arrays = refs[:asked], refs[asked : asked + operands]
    left = refs[asked + operands : asked + operands + 3 * parts]
    outs = refs[asked + operands + 3 * parts :]
    counts = counts_of(arrays, groups, rows)
    windows = [window_of(tile, tiles, groups) for tile in range(tiles)]
    block = len(layout) * tokens

    def scored(head, tile):
        return products(
            asked_of(queries, layout, first + head, tile, tokens, rows),
            gather(arrays, groups, windows[tile], 0, tokens, head),
        )

    def early(head, tile):
        share = block // parts
        at = pl.ds(aligned((head * tiles + tile) * share, share), share)
        return [jnp.concatenate([ref[at, :] for ref in left[which::3]], 0) for which in range(3)]

    def write(head, tile, result):
        for frame in range(len(layout)):
            outs[frame][pl.ds(tile * tokens, tokens), features(head)] = result[
                frame * tokens : (frame + 1) * tokens
            ]

    token = lax.broadcasted_iota(jnp.int32, (tokens, HEAD_DIM), 0)
    row = (token // TILE_W % TILE_H).astype(jnp.float32)
    real = [
        [jnp.where(row < count[n : n + 1], 1.0, 0.0).astype(jnp.bfloat16) for n in range(tiles)]
        for count in counts
    ]
    worst = jnp.zeros((block, HEAD_DIM), jnp.float32)
    for head in range(heads):
        for tile, window in enumerate(windows):
            largest, total, summed = early(head, tile)
            scores = scored(head, tile)
            largest = jnp.concatenate([largest] * (scores.shape[1] // HEAD_DIM), 1)
            weight = jnp.exp2((scores - largest) * SCALE).astype(jnp.bfloat16)
            kept = jnp.concatenate(
                [real[group][n] for group, n in window for _ in groups[group][1]], 0
            )
            values = gather(arrays, groups, window, rows, tokens, head) * kept
            added = jnp.dot(
                weight,
                jnp.concatenate([values, kept], 1),
                preferred_element_type=jnp.float32,
            )
            total = total + added[:, HEAD_DIM:]
            worst = jnp.where(total < LARGEST_TOTAL, worst, 1.0)
            result = (summed + added[:, :HEAD_DIM]) / total
            write(head, tile, result.astype(jnp.bfloat16))

    @pl.when(jnp.max(worst) > 0.0)
    def _():
        def one_head(head, _):
            for tile, window in enumerate(windows):
                before, total, summed = early(head, tile)
                scores = scored(head, tile) + bias_of(counts, groups, window, tokens)
                largest = jnp.maximum(before[:, :1], jnp.max(scores, axis=1, keepdims=True))
                shrink = jnp.exp2((before - largest) * SCALE)
                weight = jnp.exp2((scores - largest) * SCALE)
                total = jnp.sum(weight, axis=1, keepdims=True) + total * shrink
                added = jnp.dot(
                    weight.astype(jnp.bfloat16),
                    gather(arrays, groups, window, rows, tokens, head),
                    preferred_element_type=jnp.float32,
                )
                result = (added + summed * shrink) / total
                write(head, tile, result.astype(jnp.bfloat16))
            return 0

        lax.fori_loop(0, heads, one_head, 0)


def attend(kernel, operands, outs, flops=0):
    return pl.pallas_call(
        kernel,
        out_shape=outs,
        in_specs=in_vmem(len(operands)),
        out_specs=in_vmem(len(outs)),
        compiler_params=pltpu.CompilerParams(vmem_limit_bytes=VMEM_LIMIT),
        cost_estimate=pl.CostEstimate(flops=flops, bytes_accessed=0, transcendentals=0),
    )(*operands)


def attend_early(queries, jobs, arrays, groups, tiles, tokens):
    outs = [
        pltpu.VMEM((len(heads) * tiles * len(layout) * tokens, HEAD_DIM), jnp.float32)
        for layout, heads in jobs
        for _ in range(3)
    ]
    kernel = functools.partial(
        early_body, groups, len(arrays), jobs, len(queries), tiles, tokens
    )
    return attend(kernel, [*queries, *arrays], outs, EARLY_FLOPS)


def attend_late(queries, layout, arrays, groups, tiles, tokens, heads, first, left):
    outs = [pltpu.VMEM((tiles * tokens, heads * HEAD_DIM), jnp.bfloat16)] * len(layout)
    kernel = functools.partial(
        late_body, groups, len(arrays), layout, len(queries), tiles, tokens, heads, first, len(left) // 3
    )
    return attend(kernel, [*queries, *arrays, *left], outs)


def join_body(jobs, part, me_ref, *rest):
    out_ref, sems = rest[-2:]
    me = me_ref[0]
    copies = []
    for i, (bit, base) in enumerate(jobs):
        lanes = pl.ds(pl.multiple_of((me ^ bit) * part + base, HEAD_DIM), rest[i].shape[1])
        copies.append(pltpu.make_async_copy(rest[i], out_ref.at[:, lanes], sems.at[i]))
    for copy in copies:
        copy.start()
    for copy in copies:
        copy.wait()


def join(me, pieces, rows, part, devices):
    jobs = [piece[:2] for piece in pieces]
    return pl.pallas_call(
        functools.partial(join_body, jobs, part),
        out_shape=jax.ShapeDtypeStruct((rows, devices * part), jnp.bfloat16),
        in_specs=[pl.BlockSpec(memory_space=pltpu.SMEM)] + in_vmem(len(pieces)),
        out_specs=pl.BlockSpec(memory_space=pl.ANY),
        scratch_shapes=[pltpu.SemaphoreType.DMA((len(pieces),))],
        compiler_params=pltpu.CompilerParams(vmem_limit_bytes=VMEM_LIMIT),
    )(me, *(piece[2] for piece in pieces))


def body(query, key, value, valid_rows):
    devices = lax.axis_size("head")
    columns = lax.axis_size("tok")
    height = columns // TIME_TILES
    tiles, tokens, width = query.shape
    heads = width // HEAD_DIM // devices
    me = lax.axis_index("head").astype(jnp.int32).reshape(1)
    flat = [field.reshape(tiles * tokens, width) for field in (query, key, value)]
    own, sibling, passed, own_query, far, last = pack(me, valid_rows, *flat, devices)
    rows = tiles * tokens

    def by_height(block):
        if height == 1:
            return [block]
        return [block] + [swap_pairs(block, phase, 1, height, columns) for phase in (0, 1)]

    def by_time(blocks):
        return [
            swap_pairs(b, phase, height, TIME_TILES, columns) for phase in (0, 1) for b in blocks
        ]

    sibling = swap_head(sibling, 1, devices)
    passed = swap_head(passed, 1, devices)
    far = [swap_head(b, bit, devices) for bit, b in enumerate(far, 2)]
    near = by_height(stack([own, sibling], [(0, own.shape[0]), (0, 2 * rows)]))
    near = near + by_time(near)

    unit = (heads + 2) * rows
    last = [
        swap_head(stack([b, passed], [(0, unit), (i * unit, unit)]), 2 * i + 2, devices)
        for i, b in enumerate(last)
    ]
    queries = [own_query, sibling, *last]
    layout = [(0, 0, False), (1, 2 * rows, False)]
    layout += [(2 + bit // 2, bit % 2 * unit, True) for bit in range(devices - 2)]

    ends = [(bit // 2, bit % 2 * unit + heads * rows) for bit in range(devices - 2)]
    def sent(block):
        block = by_height(block)
        return block[1:] + by_time(block)

    first_heads, last_head = tuple(range(heads - 1)), (heads - 1,)
    across = sent(stack(far, [(0, 2 * rows)] * len(far), FIRST_FLOPS))
    near_groups = [(i, [[(i, 0, 0)], [(i, own.shape[0], 0)]]) for i in range(len(near))]
    own_fields = [[(len(near) + bit, 0, 0)] for bit in range(len(far))]
    groups = [(0, near_groups[0][1] + own_fields), *near_groups[1:]]
    close = attend_early(
        queries[:2], [(layout[:2], first_heads)], near + far, groups, tiles, tokens
    )

    spans = [(base, 2 * rows) for _, base in ends]
    across_last = sent(stack([last[i] for i, _ in ends], spans, after=close[:1]))
    for field, (i, base) in zip(own_fields, ends):
        field.append((len(near) + len(far) + i, base, heads - 1))
    jobs = [(layout[2:], first_heads), (layout, last_head)]
    groups = [(0, near_groups[0][1] + own_fields), *near_groups[1:]]
    left = attend_early(queries, jobs, near + far + last, groups, tiles, tokens)
    left = [[*close, *left[:3]], left[3:]]

    pieces = []
    for others, heads_now in ((across, first_heads), (across_last, last_head)):
        first = heads_now[0]
        groups = [
            (i, [[(len(others) + i, 2 * rows * bit, 0)] for bit in range(devices - 2)])
            for i in range(len(others))
        ]
        results = attend_late(
            queries,
            layout,
            near[1:] + others,
            groups,
            tiles,
            tokens,
            len(heads_now),
            first,
            left[len(pieces) > 0],
        )
        results = list(results)
        results[1] = swap_head(results[1], 1, devices)
        if not pieces:
            results[1], *left[1] = lax.optimization_barrier((results[1], *left[1]))
        pieces += [
            (bit, first * HEAD_DIM, swap_head(b, bit, devices) if bit > 1 else b)
            for bit, b in enumerate(results)
        ]
    return join(me, pieces, rows, heads * HEAD_DIM, devices).reshape(tiles, tokens, width)


def solution(mesh):
    placed = (
        P(("clips", "tok"), "head", None),
        P(("clips", "tok"), "head", None),
        P(("clips", "tok"), "head", None),
        P(("clips", "tok")),
    )
    return jax.shard_map(
        body,
        mesh=mesh,
        in_specs=placed,
        out_specs=P(("clips", "tok"), "head", None),
        check_vma=False,
    )
```

```python
import functools
import math

import jax
import jax.numpy as jnp
from jax import lax
from jax.experimental import pallas as pl
from jax.experimental.pallas import tpu as pltpu
from jax.sharding import PartitionSpec as P

HEAD_DIM = 128
TILE_H = 8
TILE_W = 8
TIME_TILES = 4
COUNT_ROWS = 16
MASKED = -1e30
LARGEST_TOTAL = 2.0**100
SCALE = math.log2(math.e) / math.sqrt(HEAD_DIM)
VMEM_LIMIT = 24 * 2**20
FIRST_FLOPS = 2500000000
EARLY_FLOPS = 0


def in_vmem(count):
    return [pl.BlockSpec(memory_space=pltpu.VMEM)] * count


def swap_head(block, bit, devices):
    return lax.ppermute(block, "head", [(i, i ^ bit) for i in range(devices)])


def swap_pairs(block, phase, stride, length, devices):
    route = []
    for i in range(devices):
        place = i // stride % length
        if place % 2 == phase and place + 1 < length:
            route += [(i, i + stride), (i + stride, i)]
    return lax.ppermute(block, "tok", route)


def pack_body(devices, heads, counts_in, me_ref, q_ref, k_ref, v_ref, *rest):
    far = devices - 2
    own_ref, sibling_ref, passed_ref, own_q_ref = rest[:4]
    far_refs, last_refs = rest[4 : 4 + far], rest[4 + far : -3]
    counts_ref, count_sem, sems = rest[-3:]
    rows = k_ref.shape[0]
    me = me_ref[0]

    def lanes(bit, first=0, count=heads):
        start = ((me ^ bit) * heads + first) * HEAD_DIM
        return pl.ds(pl.multiple_of(start, HEAD_DIM), count * HEAD_DIM)

    count_copy = pltpu.make_async_copy(counts_in, counts_ref, count_sem)
    count_copy.start()
    jobs = [
        (k_ref.at[:, lanes(1)], sibling_ref.at[pl.ds(0, rows)]),
        (v_ref.at[:, lanes(1)], sibling_ref.at[pl.ds(rows, rows)]),
        (q_ref.at[:, lanes(1)], sibling_ref.at[pl.ds(2 * rows, rows)]),
    ]
    for bit, ref in enumerate(far_refs, 2):
        jobs += [
            (k_ref.at[:, lanes(bit, 0, heads - 1)], ref.at[pl.ds(0, rows)]),
            (v_ref.at[:, lanes(bit, 0, heads - 1)], ref.at[pl.ds(rows, rows)]),
        ]
    jobs += [
        (k_ref.at[:, lanes(0)], own_ref.at[pl.ds(0, rows)]),
        (v_ref.at[:, lanes(0)], own_ref.at[pl.ds(rows, rows)]),
        (q_ref.at[:, lanes(0)], own_q_ref),
    ]
    for bit in range(2, devices):
        pair = bit // 2 - 1
        ref, base = (passed_ref, pair * (heads + 2)) if bit % 2 else (last_refs[pair], 0)
        sources = [q_ref.at[:, lanes(bit, head, 1)] for head in range(heads)]
        sources += [k_ref.at[:, lanes(bit, heads - 1, 1)], v_ref.at[:, lanes(bit, heads - 1, 1)]]
        jobs += [
            (source, ref.at[pl.ds((base + i) * rows, rows)]) for i, source in enumerate(sources)
        ]
    copies = [pltpu.make_async_copy(src, dst, sems.at[i]) for i, (src, dst) in enumerate(jobs)]
    for copy in copies:
        copy.start()
    count_copy.wait()
    shape = (COUNT_ROWS, own_ref.shape[1])
    row = lax.broadcasted_iota(jnp.int32, shape, 0)
    filled = jnp.zeros(shape, jnp.float32)
    for tile in range(counts_ref.shape[0]):
        filled = jnp.where(row == tile, counts_ref[tile].astype(jnp.float32), filled)
    own_ref[pl.ds(2 * rows, COUNT_ROWS), :] = filled.astype(jnp.bfloat16)
    for copy in copies:
        copy.wait()


def pack(me, counts, query, key, value, devices):
    rows, width = query.shape
    part = width // devices
    heads = part // HEAD_DIM
    far = devices - 2
    shapes = [(2 * rows + COUNT_ROWS, part), (3 * rows, part)]
    shapes += [(far // 2 * (heads + 2) * rows, HEAD_DIM), (rows, part)]
    shapes += [(2 * rows, part - HEAD_DIM)] * far + [((heads + 2) * rows, HEAD_DIM)] * (far // 2)
    fields = [pltpu.with_memory_space_constraint(f, pltpu.HBM) for f in (query, key, value)]
    results = pl.pallas_call(
        functools.partial(pack_body, devices, heads),
        out_shape=[pltpu.VMEM(shape, jnp.bfloat16) for shape in shapes],
        in_specs=[pl.BlockSpec(memory_space=pltpu.HBM), pl.BlockSpec(memory_space=pltpu.SMEM)]
        + [pl.BlockSpec(memory_space=pltpu.HBM)] * 3,
        out_specs=in_vmem(len(shapes)),
        scratch_shapes=[
            pltpu.SMEM(counts.shape, jnp.int32),
            pltpu.SemaphoreType.DMA,
            pltpu.SemaphoreType.DMA((6 + far * (heads + 4),)),
        ],
        compiler_params=pltpu.CompilerParams(vmem_limit_bytes=VMEM_LIMIT),
        cost_estimate=pl.CostEstimate(flops=0, bytes_accessed=12 * query.size, transcendentals=0),
    )(pltpu.with_memory_space_constraint(counts, pltpu.HBM), me, *fields)
    return (*results[:4], results[4 : 4 + far], results[4 + far :])


def stack_body(jobs, after, *refs):
    blocks, out_ref, sems = refs[: -2 - after], refs[-2], refs[-1]
    copies, base = [], 0
    for i, (first, size) in enumerate(jobs):
        source = blocks[i].at[pl.ds(first, size)]
        copies.append(
            pltpu.make_async_copy(source, out_ref.at[pl.ds(base, size)], sems.at[i])
        )
        base += size
    for copy in copies:
        copy.start()
    for copy in copies:
        copy.wait()


def stack(blocks, spans, flops=0, after=()):
    width = blocks[0].shape[1]
    rows = sum(size for _, size in spans)
    return pl.pallas_call(
        functools.partial(stack_body, spans, len(after)),
        out_shape=pltpu.VMEM((rows, width), jnp.bfloat16),
        in_specs=in_vmem(len(blocks) + len(after)),
        out_specs=pl.BlockSpec(memory_space=pltpu.VMEM),
        scratch_shapes=[pltpu.SemaphoreType.DMA((len(blocks),))],
        compiler_params=pltpu.CompilerParams(vmem_limit_bytes=VMEM_LIMIT),
        cost_estimate=pl.CostEstimate(
            flops=flops, bytes_accessed=rows * width, transcendentals=0
        ),
    )(*blocks, *after)


def features(head):
    return pl.ds(aligned(head * HEAD_DIM, HEAD_DIM), HEAD_DIM)


def window_of(tile, tiles, groups):
    near = range(max(tile - 1, 0), min(tile + 2, tiles))
    return [(group, other) for other in near for group in range(len(groups))]


def aligned(start, unit):
    return start if isinstance(start, int) else pl.multiple_of(start, unit)


def gather(arrays, groups, window, start, tokens, head):
    blocks = []
    for group, other in window:
        for field in groups[group][1]:
            index, base, first = field[0]
            for segment in field[1:]:
                if head >= segment[2]:
                    index, base, first = segment
            rows = pl.ds(base + start + other * tokens, tokens)
            blocks.append(arrays[index][rows, features(head - first)])
    return jnp.concatenate(blocks, 0)


def asked_of(queries, layout, head, tile, tokens, rows):
    blocks = []
    for index, base, by_rows in layout:
        if by_rows:
            at = pl.ds(aligned(base + head * rows + tile * tokens, tokens), tokens)
            blocks.append(queries[index][at, :])
        else:
            blocks.append(queries[index][pl.ds(base + tile * tokens, tokens), features(head)])
    return jnp.concatenate(blocks, 0)


def counts_of(arrays, groups, rows):
    counts = [arrays[i][pl.ds(2 * rows, COUNT_ROWS), pl.ds(0, HEAD_DIM)] for i, _ in groups]
    return [count.astype(jnp.float32) for count in counts]


def bias_of(counts, groups, window, tokens):
    lane = lax.broadcasted_iota(jnp.int32, (1, HEAD_DIM), 1)
    row = (lane // TILE_W % TILE_H).astype(jnp.float32)
    parts = []
    for group, other in window:
        part = jnp.where(row < counts[group][other : other + 1], 0.0, MASKED)
        parts += [part] * (len(groups[group][1]) * tokens // HEAD_DIM)
    return jnp.concatenate(parts, 1)


def products(queries, keys):
    return lax.dot_general(
        queries, keys, (((1,), (1,)), ((), ())), preferred_element_type=jnp.float32
    )


def early_body(groups, operands, jobs, asked, tiles, tokens, *refs):
    rows = tiles * tokens
    queries, arrays = refs[:asked], refs[asked : asked + operands]
    outs = refs[asked + operands :]
    counts = counts_of(arrays, groups, rows)
    windows = [window_of(tile, tiles, groups) for tile in range(tiles)]
    biases = [bias_of(counts, groups, window, tokens) for window in windows]

    def scored(job, head, tile):
        scores = products(
            asked_of(queries, jobs[job][0], head, tile, tokens, rows),
            gather(arrays, groups, windows[tile], 0, tokens, head),
        )
        scores = scores + biases[tile]
        return scores, jnp.max(scores, axis=1, keepdims=True)

    steps = [
        (job, head, tile)
        for job, (_, heads) in enumerate(jobs)
        for head in heads
        for tile in range(tiles)
    ]
    ahead = scored(*steps[0])
    for i, (job, head, tile) in enumerate(steps):
        scores, largest = ahead
        if i + 1 < len(steps):
            ahead = scored(*steps[i + 1])
        weight = jnp.exp2((scores - largest) * SCALE).astype(jnp.bfloat16)
        values = gather(arrays, groups, windows[tile], rows, tokens, head)
        values = jnp.concatenate([values, jnp.ones_like(values)], 1)
        summed = jnp.dot(weight, values, preferred_element_type=jnp.float32)
        layout, heads = jobs[job]
        block = len(layout) * tokens
        place = pl.ds(((head - heads[0]) * tiles + tile) * block, block)
        max_ref, total_ref, sum_ref = outs[3 * job : 3 * job + 3]
        max_ref[place, :] = jnp.broadcast_to(largest, (block, HEAD_DIM))
        sum_ref[place, :] = summed[:, :HEAD_DIM]
        total_ref[place, :] = summed[:, HEAD_DIM:]


def late_body(groups, operands, layout, asked, tiles, tokens, heads, first, parts, after, *refs):
    rows = tiles * tokens
    queries, arrays = refs[:asked], refs[asked : asked + operands]
    left = refs[asked + operands : asked + operands + 3 * parts]
    outs = refs[asked + operands + 3 * parts + after :]
    counts = counts_of(arrays, groups, rows)
    windows = [window_of(tile, tiles, groups) for tile in range(tiles)]
    block = len(layout) * tokens

    def scored(head, tile):
        return products(
            asked_of(queries, layout, first + head, tile, tokens, rows),
            gather(arrays, groups, windows[tile], 0, tokens, head),
        )

    def early(head, tile):
        share = block // parts
        at = pl.ds(aligned((head * tiles + tile) * share, share), share)
        return [jnp.concatenate([ref[at, :] for ref in left[which::3]], 0) for which in range(3)]

    def write(head, tile, result):
        for frame in range(len(layout)):
            outs[frame][pl.ds(tile * tokens, tokens), features(head)] = result[
                frame * tokens : (frame + 1) * tokens
            ]

    token = lax.broadcasted_iota(jnp.int32, (tokens, HEAD_DIM), 0)
    row = (token // TILE_W % TILE_H).astype(jnp.float32)
    real = [
        [jnp.where(row < count[n : n + 1], 1.0, 0.0).astype(jnp.bfloat16) for n in range(tiles)]
        for count in counts
    ]
    worst = jnp.zeros((block, HEAD_DIM), jnp.float32)
    steps = [(head, tile) for head in range(heads) for tile in range(tiles)]
    ahead = scored(*steps[0])
    for i, (head, tile) in enumerate(steps):
        scores, window = ahead, windows[tile]
        if i + 1 < len(steps):
            ahead = scored(*steps[i + 1])
        largest, total, summed = early(head, tile)
        largest = jnp.concatenate([largest] * (scores.shape[1] // HEAD_DIM), 1)
        weight = jnp.exp2((scores - largest) * SCALE).astype(jnp.bfloat16)
        kept = jnp.concatenate(
            [real[group][n] for group, n in window for _ in groups[group][1]], 0
        )
        values = gather(arrays, groups, window, rows, tokens, head) * kept
        added = jnp.dot(
            weight,
            jnp.concatenate([values, kept], 1),
            preferred_element_type=jnp.float32,
        )
        total = total + added[:, HEAD_DIM:]
        worst = jnp.where(total < LARGEST_TOTAL, worst, 1.0)
        result = (summed + added[:, :HEAD_DIM]) / total
        write(head, tile, result.astype(jnp.bfloat16))

    @pl.when(jnp.max(worst) > 0.0)
    def _():
        def one_head(head, _):
            for tile, window in enumerate(windows):
                before, total, summed = early(head, tile)
                scores = scored(head, tile) + bias_of(counts, groups, window, tokens)
                largest = jnp.maximum(before[:, :1], jnp.max(scores, axis=1, keepdims=True))
                shrink = jnp.exp2((before - largest) * SCALE)
                weight = jnp.exp2((scores - largest) * SCALE)
                total = jnp.sum(weight, axis=1, keepdims=True) + total * shrink
                added = jnp.dot(
                    weight.astype(jnp.bfloat16),
                    gather(arrays, groups, window, rows, tokens, head),
                    preferred_element_type=jnp.float32,
                )
                result = (added + summed * shrink) / total
                write(head, tile, result.astype(jnp.bfloat16))
            return 0

        lax.fori_loop(0, heads, one_head, 0)


def attend(kernel, operands, outs, flops=0):
    return pl.pallas_call(
        kernel,
        out_shape=outs,
        in_specs=in_vmem(len(operands)),
        out_specs=in_vmem(len(outs)),
        compiler_params=pltpu.CompilerParams(vmem_limit_bytes=VMEM_LIMIT),
        cost_estimate=pl.CostEstimate(flops=flops, bytes_accessed=0, transcendentals=0),
    )(*operands)


def attend_early(queries, jobs, arrays, groups, tiles, tokens):
    outs = [
        pltpu.VMEM((len(heads) * tiles * len(layout) * tokens, HEAD_DIM), jnp.float32)
        for layout, heads in jobs
        for _ in range(3)
    ]
    kernel = functools.partial(
        early_body, groups, len(arrays), jobs, len(queries), tiles, tokens
    )
    return attend(kernel, [*queries, *arrays], outs, EARLY_FLOPS)


def attend_late(queries, layout, arrays, groups, tiles, tokens, heads, first, left, after):
    outs = [pltpu.VMEM((tiles * tokens, heads * HEAD_DIM), jnp.bfloat16)] * len(layout)
    sizes = (len(arrays), layout, len(queries), tiles, tokens, heads, first)
    kernel = functools.partial(late_body, groups, *sizes, len(left) // 3, len(after))
    return attend(kernel, [*queries, *arrays, *left, *after], outs)


def join_body(jobs, part, me_ref, *rest):
    out_ref, sems = rest[-2:]
    me = me_ref[0]
    copies = []
    for i, (bit, base) in enumerate(jobs):
        lanes = pl.ds(pl.multiple_of((me ^ bit) * part + base, HEAD_DIM), rest[i].shape[1])
        copies.append(pltpu.make_async_copy(rest[i], out_ref.at[:, lanes], sems.at[i]))
    for copy in copies:
        copy.start()
    for copy in copies:
        copy.wait()


def join(me, pieces, rows, part, devices):
    jobs = [piece[:2] for piece in pieces]
    return pl.pallas_call(
        functools.partial(join_body, jobs, part),
        out_shape=jax.ShapeDtypeStruct((rows, devices * part), jnp.bfloat16),
        in_specs=[pl.BlockSpec(memory_space=pltpu.SMEM)] + in_vmem(len(pieces)),
        out_specs=pl.BlockSpec(memory_space=pl.ANY),
        scratch_shapes=[pltpu.SemaphoreType.DMA((len(pieces),))],
        compiler_params=pltpu.CompilerParams(vmem_limit_bytes=VMEM_LIMIT),
    )(me, *(piece[2] for piece in pieces))


def body(query, key, value, valid_rows):
    devices = lax.axis_size("head")
    columns = lax.axis_size("tok")
    height = columns // TIME_TILES
    tiles, tokens, width = query.shape
    heads = width // HEAD_DIM // devices
    me = lax.axis_index("head").astype(jnp.int32).reshape(1)
    flat = [field.reshape(tiles * tokens, width) for field in (query, key, value)]
    own, sibling, passed, own_query, far, last = pack(me, valid_rows, *flat, devices)
    rows = tiles * tokens

    def by_height(block):
        if height == 1:
            return [block]
        return [block] + [swap_pairs(block, phase, 1, height, columns) for phase in (0, 1)]

    def by_time(blocks):
        return [
            swap_pairs(b, phase, height, TIME_TILES, columns) for phase in (0, 1) for b in blocks
        ]

    sibling = swap_head(sibling, 1, devices)
    passed = swap_head(passed, 1, devices)
    far = [swap_head(b, bit, devices) for bit, b in enumerate(far, 2)]
    near = by_height(stack([own, sibling], [(0, own.shape[0]), (0, 2 * rows)]))
    near = near + by_time(near)

    unit = (heads + 2) * rows
    last = [
        swap_head(stack([b, passed], [(0, unit), (i * unit, unit)]), 2 * i + 2, devices)
        for i, b in enumerate(last)
    ]
    queries = [own_query, sibling, *last]
    layout = [(0, 0, False), (1, 2 * rows, False)]
    layout += [(2 + bit // 2, bit % 2 * unit, True) for bit in range(devices - 2)]

    ends = [(bit // 2, bit % 2 * unit + heads * rows) for bit in range(devices - 2)]
    def sent(block):
        block = by_height(block)
        return block[1:] + by_time(block)

    first_heads, last_head = tuple(range(heads - 1)), (heads - 1,)
    across = sent(stack(far, [(0, 2 * rows)] * len(far), FIRST_FLOPS))
    near_groups = [(i, [[(i, 0, 0)], [(i, own.shape[0], 0)]]) for i in range(len(near))]
    own_fields = [[(len(near) + bit, 0, 0)] for bit in range(len(far))]
    groups = [(0, near_groups[0][1] + own_fields), *near_groups[1:]]
    close = attend_early(
        queries[:2], [(layout[:2], first_heads)], near + far, groups, tiles, tokens
    )

    spans = [(base, 2 * rows) for _, base in ends]
    across_last = sent(stack([last[i] for i, _ in ends], spans, after=close[:1]))
    for field, (i, base) in zip(own_fields, ends):
        field.append((len(near) + len(far) + i, base, heads - 1))
    jobs = [(layout[2:], first_heads), (layout, last_head)]
    groups = [(0, near_groups[0][1] + own_fields), *near_groups[1:]]
    left = attend_early(queries, jobs, near + far + last, groups, tiles, tokens)
    left = [[*close, *left[:3]], left[3:]]

    pieces = []
    for others, heads_now in ((across, first_heads), (across_last, last_head)):
        first = heads_now[0]
        groups = [
            (i, [[(len(others) + i, 2 * rows * bit, 0)] for bit in range(devices - 2)])
            for i in range(len(others))
        ]
        results = attend_late(
            queries,
            layout,
            near[1:] + others,
            groups,
            tiles,
            tokens,
            len(heads_now),
            first,
            left[len(pieces) > 0],
            [piece[2] for piece in pieces[:1]],
        )
        pieces += [
            (bit, first * HEAD_DIM, swap_head(b, bit, devices) if bit else b)
            for bit, b in enumerate(results)
        ]
    return join(me, pieces, rows, heads * HEAD_DIM, devices).reshape(tiles, tokens, width)


def solution(mesh):
    placed = (
        P(("clips", "tok"), "head", None),
        P(("clips", "tok"), "head", None),
        P(("clips", "tok"), "head", None),
        P(("clips", "tok")),
    )
    return jax.shard_map(
        body,
        mesh=mesh,
        in_specs=placed,
        out_specs=P(("clips", "tok"), "head", None),
        check_vma=False,
    )
```

```python
import functools
import math

import jax
import jax.numpy as jnp
from jax import lax
from jax.experimental import pallas as pl
from jax.experimental.pallas import tpu as pltpu
from jax.sharding import PartitionSpec as P

HEAD_DIM = 128
TILE_H = 8
TILE_W = 8
TIME_TILES = 4
COUNT_ROWS = 16
MASKED = -1e30
LARGEST_TOTAL = 2.0**100
SCALE = math.log2(math.e) / math.sqrt(HEAD_DIM)
VMEM_LIMIT = 24 * 2**20
FIRST_FLOPS = 2500000000
EARLY_FLOPS = 0


def in_vmem(count):
    return [pl.BlockSpec(memory_space=pltpu.VMEM)] * count


def swap_head(block, bit, devices):
    return lax.ppermute(block, "head", [(i, i ^ bit) for i in range(devices)])


def swap_pairs(block, phase, stride, length, devices):
    route = []
    for i in range(devices):
        place = i // stride % length
        if place % 2 == phase and place + 1 < length:
            route += [(i, i + stride), (i + stride, i)]
    return lax.ppermute(block, "tok", route)


def pack_body(devices, heads, counts_in, me_ref, q_ref, k_ref, v_ref, *rest):
    far = devices - 2
    own_ref, sibling_ref, passed_ref, own_q_ref = rest[:4]
    far_refs, last_refs = rest[4 : 4 + far], rest[4 + far : -3]
    counts_ref, count_sem, sems = rest[-3:]
    rows = k_ref.shape[0]
    me = me_ref[0]

    def lanes(bit, first=0, count=heads):
        start = ((me ^ bit) * heads + first) * HEAD_DIM
        return pl.ds(pl.multiple_of(start, HEAD_DIM), count * HEAD_DIM)

    count_copy = pltpu.make_async_copy(counts_in, counts_ref, count_sem)
    count_copy.start()
    jobs = [
        (k_ref.at[:, lanes(1)], sibling_ref.at[pl.ds(0, rows)]),
        (v_ref.at[:, lanes(1)], sibling_ref.at[pl.ds(rows, rows)]),
        (q_ref.at[:, lanes(1)], sibling_ref.at[pl.ds(2 * rows, rows)]),
    ]
    for bit, ref in enumerate(far_refs, 2):
        jobs += [
            (k_ref.at[:, lanes(bit, 0, heads - 1)], ref.at[pl.ds(0, rows)]),
            (v_ref.at[:, lanes(bit, 0, heads - 1)], ref.at[pl.ds(rows, rows)]),
        ]
    jobs += [
        (k_ref.at[:, lanes(0)], own_ref.at[pl.ds(0, rows)]),
        (v_ref.at[:, lanes(0)], own_ref.at[pl.ds(rows, rows)]),
        (q_ref.at[:, lanes(0)], own_q_ref),
    ]
    for bit in range(2, devices):
        pair = bit // 2 - 1
        ref, base = (passed_ref, pair * (heads + 2)) if bit % 2 else (last_refs[pair], 0)
        sources = [q_ref.at[:, lanes(bit, head, 1)] for head in range(heads)]
        sources += [k_ref.at[:, lanes(bit, heads - 1, 1)], v_ref.at[:, lanes(bit, heads - 1, 1)]]
        jobs += [
            (source, ref.at[pl.ds((base + i) * rows, rows)]) for i, source in enumerate(sources)
        ]
    copies = [pltpu.make_async_copy(src, dst, sems.at[i]) for i, (src, dst) in enumerate(jobs)]
    for copy in copies:
        copy.start()
    count_copy.wait()
    shape = (COUNT_ROWS, own_ref.shape[1])
    row = lax.broadcasted_iota(jnp.int32, shape, 0)
    filled = jnp.zeros(shape, jnp.float32)
    for tile in range(counts_ref.shape[0]):
        filled = jnp.where(row == tile, counts_ref[tile].astype(jnp.float32), filled)
    own_ref[pl.ds(2 * rows, COUNT_ROWS), :] = filled.astype(jnp.bfloat16)
    for copy in copies:
        copy.wait()


def pack(me, counts, query, key, value, devices):
    rows, width = query.shape
    part = width // devices
    heads = part // HEAD_DIM
    far = devices - 2
    shapes = [(2 * rows + COUNT_ROWS, part), (3 * rows, part)]
    shapes += [(far // 2 * (heads + 2) * rows, HEAD_DIM), (rows, part)]
    shapes += [(2 * rows, part - HEAD_DIM)] * far + [((heads + 2) * rows, HEAD_DIM)] * (far // 2)
    fields = [pltpu.with_memory_space_constraint(f, pltpu.HBM) for f in (query, key, value)]
    results = pl.pallas_call(
        functools.partial(pack_body, devices, heads),
        out_shape=[pltpu.VMEM(shape, jnp.bfloat16) for shape in shapes],
        in_specs=[pl.BlockSpec(memory_space=pltpu.HBM), pl.BlockSpec(memory_space=pltpu.SMEM)]
        + [pl.BlockSpec(memory_space=pltpu.HBM)] * 3,
        out_specs=in_vmem(len(shapes)),
        scratch_shapes=[
            pltpu.SMEM(counts.shape, jnp.int32),
            pltpu.SemaphoreType.DMA,
            pltpu.SemaphoreType.DMA((6 + far * (heads + 4),)),
        ],
        compiler_params=pltpu.CompilerParams(vmem_limit_bytes=VMEM_LIMIT),
        cost_estimate=pl.CostEstimate(flops=0, bytes_accessed=12 * query.size, transcendentals=0),
    )(pltpu.with_memory_space_constraint(counts, pltpu.HBM), me, *fields)
    return (*results[:4], results[4 : 4 + far], results[4 + far :])


def stack_body(jobs, after, *refs):
    blocks, out_ref, sems = refs[: -2 - after], refs[-2], refs[-1]
    copies, base = [], 0
    for i, (first, size) in enumerate(jobs):
        source = blocks[i].at[pl.ds(first, size)]
        copies.append(
            pltpu.make_async_copy(source, out_ref.at[pl.ds(base, size)], sems.at[i])
        )
        base += size
    for copy in copies:
        copy.start()
    for copy in copies:
        copy.wait()


def stack(blocks, spans, flops=0, after=()):
    width = blocks[0].shape[1]
    rows = sum(size for _, size in spans)
    return pl.pallas_call(
        functools.partial(stack_body, spans, len(after)),
        out_shape=pltpu.VMEM((rows, width), jnp.bfloat16),
        in_specs=in_vmem(len(blocks) + len(after)),
        out_specs=pl.BlockSpec(memory_space=pltpu.VMEM),
        scratch_shapes=[pltpu.SemaphoreType.DMA((len(blocks),))],
        compiler_params=pltpu.CompilerParams(vmem_limit_bytes=VMEM_LIMIT),
        cost_estimate=pl.CostEstimate(
            flops=flops, bytes_accessed=rows * width, transcendentals=0
        ),
    )(*blocks, *after)


def features(head):
    return pl.ds(aligned(head * HEAD_DIM, HEAD_DIM), HEAD_DIM)


def window_of(tile, tiles, groups):
    near = range(max(tile - 1, 0), min(tile + 2, tiles))
    return [(group, other) for other in near for group in range(len(groups))]


def aligned(start, unit):
    return start if isinstance(start, int) else pl.multiple_of(start, unit)


def gather(arrays, groups, window, start, tokens, head):
    blocks = []
    for group, other in window:
        for field in groups[group][1]:
            index, base, first = field[0]
            for segment in field[1:]:
                if head >= segment[2]:
                    index, base, first = segment
            rows = pl.ds(base + start + other * tokens, tokens)
            blocks.append(arrays[index][rows, features(head - first)])
    return jnp.concatenate(blocks, 0)


def asked_of(queries, layout, head, tile, tokens, rows):
    blocks = []
    for index, base, by_rows in layout:
        if by_rows:
            at = pl.ds(aligned(base + head * rows + tile * tokens, tokens), tokens)
            blocks.append(queries[index][at, :])
        else:
            blocks.append(queries[index][pl.ds(base + tile * tokens, tokens), features(head)])
    return jnp.concatenate(blocks, 0)


def counts_of(arrays, groups, rows):
    counts = [arrays[i][pl.ds(2 * rows, COUNT_ROWS), pl.ds(0, HEAD_DIM)] for i, _ in groups]
    return [count.astype(jnp.float32) for count in counts]


def bias_of(counts, groups, window, tokens):
    lane = lax.broadcasted_iota(jnp.int32, (1, HEAD_DIM), 1)
    row = (lane // TILE_W % TILE_H).astype(jnp.float32)
    parts = []
    for group, other in window:
        part = jnp.where(row < counts[group][other : other + 1], 0.0, MASKED)
        parts += [part] * (len(groups[group][1]) * tokens // HEAD_DIM)
    return jnp.concatenate(parts, 1)


def products(queries, keys):
    return lax.dot_general(
        queries, keys, (((1,), (1,)), ((), ())), preferred_element_type=jnp.float32
    )


def early_body(groups, operands, jobs, asked, tiles, tokens, *refs):
    rows = tiles * tokens
    queries, arrays = refs[:asked], refs[asked : asked + operands]
    outs = refs[asked + operands :]
    counts = counts_of(arrays, groups, rows)
    windows = [window_of(tile, tiles, groups) for tile in range(tiles)]
    biases = [bias_of(counts, groups, window, tokens) for window in windows]

    def scored(job, head, tile):
        scores = products(
            asked_of(queries, jobs[job][0], head, tile, tokens, rows),
            gather(arrays, groups, windows[tile], 0, tokens, head),
        )
        scores = scores + biases[tile]
        return scores, jnp.max(scores, axis=1, keepdims=True)

    steps = [
        (job, head, tile)
        for job, (_, heads) in enumerate(jobs)
        for head in heads
        for tile in range(tiles)
    ]
    ahead = scored(*steps[0])
    for i, (job, head, tile) in enumerate(steps):
        scores, largest = ahead
        if i + 1 < len(steps):
            ahead = scored(*steps[i + 1])
        weight = jnp.exp2((scores - largest) * SCALE).astype(jnp.bfloat16)
        values = gather(arrays, groups, windows[tile], rows, tokens, head)
        values = jnp.concatenate([values, jnp.ones_like(values)], 1)
        summed = jnp.dot(weight, values, preferred_element_type=jnp.float32)
        layout, heads = jobs[job]
        block = len(layout) * tokens
        place = pl.ds(((head - heads[0]) * tiles + tile) * block, block)
        max_ref, total_ref, sum_ref = outs[3 * job : 3 * job + 3]
        max_ref[place, :] = jnp.broadcast_to(largest, (block, HEAD_DIM))
        sum_ref[place, :] = summed[:, :HEAD_DIM]
        total_ref[place, :] = summed[:, HEAD_DIM:]


def late_body(groups, operands, layout, asked, tiles, tokens, heads, first, parts, after, *refs):
    rows = tiles * tokens
    queries, arrays = refs[:asked], refs[asked : asked + operands]
    left = refs[asked + operands : asked + operands + 3 * parts]
    outs = refs[asked + operands + 3 * parts + after :]
    counts = counts_of(arrays, groups, rows)
    windows = [window_of(tile, tiles, groups) for tile in range(tiles)]
    block = len(layout) * tokens

    def scored(head, tile):
        return products(
            asked_of(queries, layout, first + head, tile, tokens, rows),
            gather(arrays, groups, windows[tile], 0, tokens, head),
        )

    def early(head, tile):
        share = block // parts
        at = pl.ds(aligned((head * tiles + tile) * share, share), share)
        return [jnp.concatenate([ref[at, :] for ref in left[which::3]], 0) for which in range(3)]

    def write(head, tile, result):
        for frame in range(len(layout)):
            outs[frame][pl.ds(tile * tokens, tokens), features(head)] = result[
                frame * tokens : (frame + 1) * tokens
            ]

    token = lax.broadcasted_iota(jnp.int32, (tokens, HEAD_DIM), 0)
    row = (token // TILE_W % TILE_H).astype(jnp.float32)
    real = [
        [jnp.where(row < count[n : n + 1], 1.0, 0.0).astype(jnp.bfloat16) for n in range(tiles)]
        for count in counts
    ]
    worst = jnp.zeros((block, HEAD_DIM), jnp.float32)
    steps = [(head, tile) for head in range(heads) for tile in range(tiles)]
    ahead = scored(*steps[0])
    for i, (head, tile) in enumerate(steps):
        scores, window = ahead, windows[tile]
        if i + 1 < len(steps):
            ahead = scored(*steps[i + 1])
        largest, total, summed = early(head, tile)
        largest = jnp.concatenate([largest] * (scores.shape[1] // HEAD_DIM), 1)
        weight = jnp.exp2((scores - largest) * SCALE).astype(jnp.bfloat16)
        kept = jnp.concatenate(
            [real[group][n] for group, n in window for _ in groups[group][1]], 0
        )
        values = gather(arrays, groups, window, rows, tokens, head) * kept
        added = jnp.dot(
            weight,
            jnp.concatenate([values, kept], 1),
            preferred_element_type=jnp.float32,
        )
        total = total + added[:, HEAD_DIM:]
        worst = jnp.where(total < LARGEST_TOTAL, worst, 1.0)
        result = (summed + added[:, :HEAD_DIM]) / total
        write(head, tile, result.astype(jnp.bfloat16))

    @pl.when(jnp.max(worst) > 0.0)
    def _():
        def one_head(head, _):
            for tile, window in enumerate(windows):
                before, total, summed = early(head, tile)
                scores = scored(head, tile) + bias_of(counts, groups, window, tokens)
                largest = jnp.maximum(before[:, :1], jnp.max(scores, axis=1, keepdims=True))
                shrink = jnp.exp2((before - largest) * SCALE)
                weight = jnp.exp2((scores - largest) * SCALE)
                total = jnp.sum(weight, axis=1, keepdims=True) + total * shrink
                added = jnp.dot(
                    weight.astype(jnp.bfloat16),
                    gather(arrays, groups, window, rows, tokens, head),
                    preferred_element_type=jnp.float32,
                )
                result = (added + summed * shrink) / total
                write(head, tile, result.astype(jnp.bfloat16))
            return 0

        lax.fori_loop(0, heads, one_head, 0)


def attend(kernel, operands, outs, flops=0):
    return pl.pallas_call(
        kernel,
        out_shape=outs,
        in_specs=in_vmem(len(operands)),
        out_specs=in_vmem(len(outs)),
        compiler_params=pltpu.CompilerParams(vmem_limit_bytes=VMEM_LIMIT),
        cost_estimate=pl.CostEstimate(flops=flops, bytes_accessed=0, transcendentals=0),
    )(*operands)


def attend_early(queries, jobs, arrays, groups, tiles, tokens):
    outs = [
        pltpu.VMEM((len(heads) * tiles * len(layout) * tokens, HEAD_DIM), jnp.float32)
        for layout, heads in jobs
        for _ in range(3)
    ]
    kernel = functools.partial(
        early_body, groups, len(arrays), jobs, len(queries), tiles, tokens
    )
    return attend(kernel, [*queries, *arrays], outs, EARLY_FLOPS)


def attend_late(queries, layout, arrays, groups, tiles, tokens, heads, first, left, after):
    outs = [pltpu.VMEM((tiles * tokens, heads * HEAD_DIM), jnp.bfloat16)] * len(layout)
    sizes = (len(arrays), layout, len(queries), tiles, tokens, heads, first)
    kernel = functools.partial(late_body, groups, *sizes, len(left) // 3, len(after))
    return attend(kernel, [*queries, *arrays, *left, *after], outs)


def join_body(jobs, part, held, me_ref, *rest):
    out_ref, sems = rest[-2:]
    rest = rest[held:]
    me = me_ref[0]
    copies = []
    for i, (bit, base) in enumerate(jobs):
        lanes = pl.ds(pl.multiple_of((me ^ bit) * part + base, HEAD_DIM), rest[i].shape[1])
        copies.append(pltpu.make_async_copy(rest[i], out_ref.at[:, lanes], sems.at[i]))
    for copy in copies:
        copy.start()
    for copy in copies:
        copy.wait()


def join(me, pieces, rows, part, devices, begun=()):
    jobs = [piece[:2] for piece in pieces]
    hbm = [pl.BlockSpec(memory_space=pltpu.HBM)]
    return pl.pallas_call(
        functools.partial(join_body, jobs, part, len(begun)),
        out_shape=jax.ShapeDtypeStruct((rows, devices * part), jnp.bfloat16),
        in_specs=[pl.BlockSpec(memory_space=pltpu.SMEM)]
        + hbm * len(begun)
        + in_vmem(len(pieces)),
        out_specs=hbm[0],
        scratch_shapes=[pltpu.SemaphoreType.DMA((len(pieces),))],
        input_output_aliases={1: 0} if begun else {},
        compiler_params=pltpu.CompilerParams(vmem_limit_bytes=VMEM_LIMIT),
    )(me, *begun, *(piece[2] for piece in pieces))


def body(query, key, value, valid_rows):
    devices = lax.axis_size("head")
    columns = lax.axis_size("tok")
    height = columns // TIME_TILES
    tiles, tokens, width = query.shape
    heads = width // HEAD_DIM // devices
    me = lax.axis_index("head").astype(jnp.int32).reshape(1)
    flat = [field.reshape(tiles * tokens, width) for field in (query, key, value)]
    own, sibling, passed, own_query, far, last = pack(me, valid_rows, *flat, devices)
    rows = tiles * tokens

    def by_height(block):
        if height == 1:
            return [block]
        return [block] + [swap_pairs(block, phase, 1, height, columns) for phase in (0, 1)]

    def by_time(blocks):
        return [
            swap_pairs(b, phase, height, TIME_TILES, columns) for phase in (0, 1) for b in blocks
        ]

    sibling = swap_head(sibling, 1, devices)
    passed = swap_head(passed, 1, devices)
    far = [swap_head(b, bit, devices) for bit, b in enumerate(far, 2)]
    near = by_height(stack([own, sibling], [(0, own.shape[0]), (0, 2 * rows)]))
    near = near + by_time(near)

    unit = (heads + 2) * rows
    last = [
        swap_head(stack([b, passed], [(0, unit), (i * unit, unit)]), 2 * i + 2, devices)
        for i, b in enumerate(last)
    ]
    queries = [own_query, sibling, *last]
    layout = [(0, 0, False), (1, 2 * rows, False)]
    layout += [(2 + bit // 2, bit % 2 * unit, True) for bit in range(devices - 2)]

    ends = [(bit // 2, bit % 2 * unit + heads * rows) for bit in range(devices - 2)]
    def sent(block):
        block = by_height(block)
        return block[1:] + by_time(block)

    first_heads, last_head = tuple(range(heads - 1)), (heads - 1,)
    across = sent(stack(far, [(0, 2 * rows)] * len(far), FIRST_FLOPS))
    near_groups = [(i, [[(i, 0, 0)], [(i, own.shape[0], 0)]]) for i in range(len(near))]
    own_fields = [[(len(near) + bit, 0, 0)] for bit in range(len(far))]
    groups = [(0, near_groups[0][1] + own_fields), *near_groups[1:]]
    close = attend_early(
        queries[:2], [(layout[:2], first_heads)], near + far, groups, tiles, tokens
    )

    spans = [(base, 2 * rows) for _, base in ends]
    across_last = sent(stack([last[i] for i, _ in ends], spans, after=close[:1]))
    for field, (i, base) in zip(own_fields, ends):
        field.append((len(near) + len(far) + i, base, heads - 1))
    jobs = [(layout[2:], first_heads), (layout, last_head)]
    groups = [(0, near_groups[0][1] + own_fields), *near_groups[1:]]
    left = attend_early(queries, jobs, near + far + last, groups, tiles, tokens)
    left = [[*close, *left[:3]], left[3:]]

    pieces = []
    for others, heads_now in ((across, first_heads), (across_last, last_head)):
        first = heads_now[0]
        groups = [
            (i, [[(len(others) + i, 2 * rows * bit, 0)] for bit in range(devices - 2)])
            for i in range(len(others))
        ]
        results = attend_late(
            queries,
            layout,
            near[1:] + others,
            groups,
            tiles,
            tokens,
            len(heads_now),
            first,
            left[len(pieces) > 0],
            [piece[2] for piece in pieces[:1]],
        )
        order = range(devices) if not pieces else range(devices - 1, -1, -1)
        pieces += [
            (bit, first * HEAD_DIM, swap_head(results[bit], bit, devices) if bit else results[0])
            for bit in order
        ]
    begun, ended = [], []
    for piece in pieces:
        (ended if piece[0] and piece[1] else begun).append(piece)
    shape = (rows, heads * HEAD_DIM, devices)
    joined = join(me, ended, *shape, [join(me, begun, *shape)])
    return joined.reshape(tiles, tokens, width)


def solution(mesh):
    placed = (
        P(("clips", "tok"), "head", None),
        P(("clips", "tok"), "head", None),
        P(("clips", "tok"), "head", None),
        P(("clips", "tok")),
    )
    return jax.shard_map(
        body,
        mesh=mesh,
        in_specs=placed,
        out_specs=P(("clips", "tok"), "head", None),
        check_vma=False,
    )
```

```python
import functools
import math

import jax
import jax.numpy as jnp
from jax import lax
from jax.experimental import pallas as pl
from jax.experimental.pallas import tpu as pltpu
from jax.sharding import PartitionSpec as P

HEAD_DIM = 128
TILE_H = 8
TILE_W = 8
TIME_TILES = 4
COUNT_ROWS = 16
MASKED = -1e30
LARGEST_TOTAL = 2.0**100
SCALE = math.log2(math.e) / math.sqrt(HEAD_DIM)
VMEM_LIMIT = 24 * 2**20
FIRST_FLOPS = 2500000000
EARLY_FLOPS = 0


def in_vmem(count):
    return [pl.BlockSpec(memory_space=pltpu.VMEM)] * count


def swap_head(block, bit, devices):
    return lax.ppermute(block, "head", [(i, i ^ bit) for i in range(devices)])


def swap_pairs(block, phase, stride, length, devices):
    route = []
    for i in range(devices):
        place = i // stride % length
        if place % 2 == phase and place + 1 < length:
            route += [(i, i + stride), (i + stride, i)]
    return lax.ppermute(block, "tok", route)


def lanes_of(owner, heads, first=0, count=None):
    start = pl.multiple_of((owner * heads + first) * HEAD_DIM, HEAD_DIM)
    return pl.ds(start, (heads if count is None else count) * HEAD_DIM)


def run_copies(jobs, sems):
    copies = [pltpu.make_async_copy(src, dst, sems.at[i]) for i, (src, dst) in enumerate(jobs)]
    for copy in copies:
        copy.start()
    return copies


def last_of(q_ref, k_ref, v_ref, owner, heads):
    sources = [q_ref.at[:, lanes_of(owner, heads, head, 1)] for head in range(heads)]
    return sources + [ref.at[:, lanes_of(owner, heads, heads - 1, 1)] for ref in (k_ref, v_ref)]


def pack_body(devices, heads, counts_in, me_ref, q_ref, k_ref, v_ref, *rest):
    own_ref, sibling_ref, passed_ref = rest[:3]
    far_refs = rest[3:-3]
    counts_ref, count_sem, sems = rest[-3:]
    rows = k_ref.shape[0]
    me = me_ref[0]
    count_copy = pltpu.make_async_copy(counts_in, counts_ref, count_sem)
    count_copy.start()
    beside = lanes_of(me ^ 1, heads)
    jobs = [
        (ref.at[:, beside], sibling_ref.at[pl.ds(i * rows, rows)])
        for i, ref in enumerate((k_ref, v_ref, q_ref))
    ]
    for bit, far_ref in enumerate(far_refs, 2):
        jobs += [
            (ref.at[:, lanes_of(me ^ bit, heads, 0, heads - 1)], far_ref.at[pl.ds(i * rows, rows)])
            for i, ref in enumerate((k_ref, v_ref))
        ]
    jobs += [
        (ref.at[:, lanes_of(me, heads)], own_ref.at[pl.ds(i * rows, rows)])
        for i, ref in enumerate((k_ref, v_ref))
    ]
    passed = [
        source
        for bit in range(3, devices, 2)
        for source in last_of(q_ref, k_ref, v_ref, me ^ bit, heads)
    ]
    jobs += [(source, passed_ref.at[pl.ds(i * rows, rows)]) for i, source in enumerate(passed)]
    copies = run_copies(jobs, sems)
    count_copy.wait()
    shape = (COUNT_ROWS, own_ref.shape[1])
    row = lax.broadcasted_iota(jnp.int32, shape, 0)
    filled = jnp.zeros(shape, jnp.float32)
    for tile in range(counts_ref.shape[0]):
        filled = jnp.where(row == tile, counts_ref[tile].astype(jnp.float32), filled)
    own_ref[pl.ds(2 * rows, COUNT_ROWS), :] = filled.astype(jnp.bfloat16)
    for copy in copies:
        copy.wait()


def pack(me, counts, fields, devices):
    rows, width = fields[0].shape
    part = width // devices
    heads = part // HEAD_DIM
    far = devices - 2
    shapes = [(2 * rows + COUNT_ROWS, part), (3 * rows, part)]
    shapes += [(far // 2 * (heads + 2) * rows, HEAD_DIM)] + [(2 * rows, part - HEAD_DIM)] * far
    results = pl.pallas_call(
        functools.partial(pack_body, devices, heads),
        out_shape=[pltpu.VMEM(shape, jnp.bfloat16) for shape in shapes],
        in_specs=[pl.BlockSpec(memory_space=pltpu.HBM), pl.BlockSpec(memory_space=pltpu.SMEM)]
        + [pl.BlockSpec(memory_space=pltpu.HBM)] * 3,
        out_specs=in_vmem(len(shapes)),
        scratch_shapes=[
            pltpu.SMEM(counts.shape, jnp.int32),
            pltpu.SemaphoreType.DMA,
            pltpu.SemaphoreType.DMA((5 + 2 * far + far // 2 * (heads + 2),)),
        ],
        compiler_params=pltpu.CompilerParams(vmem_limit_bytes=VMEM_LIMIT),
        cost_estimate=pl.CostEstimate(
            flops=0, bytes_accessed=12 * rows * width, transcendentals=0
        ),
    )(pltpu.with_memory_space_constraint(counts, pltpu.HBM), me, *fields)
    return results[0], results[1], results[2], results[3:]


def pack_last_body(devices, heads, me_ref, q_ref, k_ref, v_ref, passed_ref, *rest):
    own_q_ref, last_refs, sems = rest[0], rest[1:-1], rest[-1]
    rows = k_ref.shape[0]
    unit = (heads + 2) * rows
    me = me_ref[0]
    jobs = [(q_ref.at[:, lanes_of(me, heads)], own_q_ref)]
    for pair, last_ref in enumerate(last_refs):
        sources = last_of(q_ref, k_ref, v_ref, me ^ (2 * pair + 2), heads)
        jobs += [(source, last_ref.at[pl.ds(i * rows, rows)]) for i, source in enumerate(sources)]
        jobs.append((passed_ref.at[pl.ds(pair * unit, unit)], last_ref.at[pl.ds(unit, unit)]))
    for copy in run_copies(jobs, sems):
        copy.wait()


def pack_last(me, fields, passed, devices):
    rows, width = fields[0].shape
    part = width // devices
    heads = part // HEAD_DIM
    far = devices // 2 - 1
    shapes = [(rows, part)] + [(2 * (heads + 2) * rows, HEAD_DIM)] * far
    results = pl.pallas_call(
        functools.partial(pack_last_body, devices, heads),
        out_shape=[pltpu.VMEM(shape, jnp.bfloat16) for shape in shapes],
        in_specs=[pl.BlockSpec(memory_space=pltpu.SMEM)]
        + [pl.BlockSpec(memory_space=pltpu.HBM)] * 3
        + in_vmem(1),
        out_specs=in_vmem(len(shapes)),
        scratch_shapes=[pltpu.SemaphoreType.DMA((1 + far * (heads + 3),))],
        compiler_params=pltpu.CompilerParams(vmem_limit_bytes=VMEM_LIMIT),
        cost_estimate=pl.CostEstimate(
            flops=0, bytes_accessed=2 * (heads + 2) * rows * HEAD_DIM, transcendentals=0
        ),
    )(me, *fields, passed)
    return results[0], results[1:]


def stack_body(jobs, after, *refs):
    blocks, out_ref, sems = refs[: -2 - after], refs[-2], refs[-1]
    copies, base = [], 0
    for i, (first, size) in enumerate(jobs):
        source = blocks[i].at[pl.ds(first, size)]
        copies.append(
            pltpu.make_async_copy(source, out_ref.at[pl.ds(base, size)], sems.at[i])
        )
        base += size
    for copy in copies:
        copy.start()
    for copy in copies:
        copy.wait()


def stack(blocks, spans, flops=0, after=()):
    width = blocks[0].shape[1]
    rows = sum(size for _, size in spans)
    return pl.pallas_call(
        functools.partial(stack_body, spans, len(after)),
        out_shape=pltpu.VMEM((rows, width), jnp.bfloat16),
        in_specs=in_vmem(len(blocks) + len(after)),
        out_specs=pl.BlockSpec(memory_space=pltpu.VMEM),
        scratch_shapes=[pltpu.SemaphoreType.DMA((len(blocks),))],
        compiler_params=pltpu.CompilerParams(vmem_limit_bytes=VMEM_LIMIT),
        cost_estimate=pl.CostEstimate(
            flops=flops, bytes_accessed=rows * width, transcendentals=0
        ),
    )(*blocks, *after)


def features(head):
    return pl.ds(aligned(head * HEAD_DIM, HEAD_DIM), HEAD_DIM)


def window_of(tile, tiles, groups):
    near = range(max(tile - 1, 0), min(tile + 2, tiles))
    return [(group, other) for other in near for group in range(len(groups))]


def aligned(start, unit):
    return start if isinstance(start, int) else pl.multiple_of(start, unit)


def gather(arrays, groups, window, start, tokens, head):
    blocks = []
    for group, other in window:
        for field in groups[group][1]:
            index, base, first = field[0]
            for segment in field[1:]:
                if head >= segment[2]:
                    index, base, first = segment
            rows = pl.ds(base + start + other * tokens, tokens)
            blocks.append(arrays[index][rows, features(head - first)])
    return jnp.concatenate(blocks, 0)


def asked_of(queries, layout, head, tile, tokens, rows):
    blocks = []
    for index, base, by_rows in layout:
        if by_rows:
            at = pl.ds(aligned(base + head * rows + tile * tokens, tokens), tokens)
            blocks.append(queries[index][at, :])
        else:
            blocks.append(queries[index][pl.ds(base + tile * tokens, tokens), features(head)])
    return jnp.concatenate(blocks, 0)


def counts_of(arrays, groups, rows):
    counts = [arrays[i][pl.ds(2 * rows, COUNT_ROWS), pl.ds(0, HEAD_DIM)] for i, _ in groups]
    return [count.astype(jnp.float32) for count in counts]


def bias_of(counts, groups, window, tokens):
    lane = lax.broadcasted_iota(jnp.int32, (1, HEAD_DIM), 1)
    row = (lane // TILE_W % TILE_H).astype(jnp.float32)
    parts = []
    for group, other in window:
        part = jnp.where(row < counts[group][other : other + 1], 0.0, MASKED)
        parts += [part] * (len(groups[group][1]) * tokens // HEAD_DIM)
    return jnp.concatenate(parts, 1)


def products(queries, keys):
    return lax.dot_general(
        queries, keys, (((1,), (1,)), ((), ())), preferred_element_type=jnp.float32
    )


def early_body(groups, operands, jobs, asked, tiles, tokens, *refs):
    rows = tiles * tokens
    queries, arrays = refs[:asked], refs[asked : asked + operands]
    outs = refs[asked + operands :]
    counts = counts_of(arrays, groups, rows)
    windows = [window_of(tile, tiles, groups) for tile in range(tiles)]
    biases = [bias_of(counts, groups, window, tokens) for window in windows]

    def scored(job, head, tile):
        scores = products(
            asked_of(queries, jobs[job][0], head, tile, tokens, rows),
            gather(arrays, groups, windows[tile], 0, tokens, head),
        )
        scores = scores + biases[tile]
        return scores, jnp.max(scores, axis=1, keepdims=True)

    steps = [
        (job, head, tile)
        for job, (_, heads) in enumerate(jobs)
        for head in heads
        for tile in range(tiles)
    ]
    ahead = scored(*steps[0])
    for i, (job, head, tile) in enumerate(steps):
        scores, largest = ahead
        if i + 1 < len(steps):
            ahead = scored(*steps[i + 1])
        weight = jnp.exp2((scores - largest) * SCALE).astype(jnp.bfloat16)
        values = gather(arrays, groups, windows[tile], rows, tokens, head)
        values = jnp.concatenate([values, jnp.ones_like(values)], 1)
        summed = jnp.dot(weight, values, preferred_element_type=jnp.float32)
        layout, heads = jobs[job]
        block = len(layout) * tokens
        place = pl.ds(((head - heads[0]) * tiles + tile) * block, block)
        max_ref, total_ref, sum_ref = outs[3 * job : 3 * job + 3]
        max_ref[place, :] = jnp.broadcast_to(largest, (block, HEAD_DIM))
        sum_ref[place, :] = summed[:, :HEAD_DIM]
        total_ref[place, :] = summed[:, HEAD_DIM:]


def late_body(groups, operands, layout, asked, tiles, tokens, heads, first, parts, after, *refs):
    rows = tiles * tokens
    queries, arrays = refs[:asked], refs[asked : asked + operands]
    left = refs[asked + operands : asked + operands + 3 * parts]
    outs = refs[asked + operands + 3 * parts + after :]
    counts = counts_of(arrays, groups, rows)
    windows = [window_of(tile, tiles, groups) for tile in range(tiles)]
    block = len(layout) * tokens

    def scored(head, tile):
        return products(
            asked_of(queries, layout, first + head, tile, tokens, rows),
            gather(arrays, groups, windows[tile], 0, tokens, head),
        )

    def early(head, tile):
        share = block // parts
        at = pl.ds(aligned((head * tiles + tile) * share, share), share)
        return [jnp.concatenate([ref[at, :] for ref in left[which::3]], 0) for which in range(3)]

    def write(head, tile, result):
        for frame in range(len(layout)):
            outs[frame][pl.ds(tile * tokens, tokens), features(head)] = result[
                frame * tokens : (frame + 1) * tokens
            ]

    token = lax.broadcasted_iota(jnp.int32, (tokens, HEAD_DIM), 0)
    row = (token // TILE_W % TILE_H).astype(jnp.float32)
    real = [
        [jnp.where(row < count[n : n + 1], 1.0, 0.0).astype(jnp.bfloat16) for n in range(tiles)]
        for count in counts
    ]
    worst = jnp.zeros((block, HEAD_DIM), jnp.float32)
    steps = [(head, tile) for head in range(heads) for tile in range(tiles)]
    ahead = scored(*steps[0])
    for i, (head, tile) in enumerate(steps):
        scores, window = ahead, windows[tile]
        if i + 1 < len(steps):
            ahead = scored(*steps[i + 1])
        largest, total, summed = early(head, tile)
        largest = jnp.concatenate([largest] * (scores.shape[1] // HEAD_DIM), 1)
        weight = jnp.exp2((scores - largest) * SCALE).astype(jnp.bfloat16)
        kept = jnp.concatenate(
            [real[group][n] for group, n in window for _ in groups[group][1]], 0
        )
        values = gather(arrays, groups, window, rows, tokens, head) * kept
        added = jnp.dot(
            weight,
            jnp.concatenate([values, kept], 1),
            preferred_element_type=jnp.float32,
        )
        total = total + added[:, HEAD_DIM:]
        worst = jnp.where(total < LARGEST_TOTAL, worst, 1.0)
        result = (summed + added[:, :HEAD_DIM]) / total
        write(head, tile, result.astype(jnp.bfloat16))

    @pl.when(jnp.max(worst) > 0.0)
    def _():
        def one_head(head, _):
            for tile, window in enumerate(windows):
                before, total, summed = early(head, tile)
                scores = scored(head, tile) + bias_of(counts, groups, window, tokens)
                largest = jnp.maximum(before[:, :1], jnp.max(scores, axis=1, keepdims=True))
                shrink = jnp.exp2((before - largest) * SCALE)
                weight = jnp.exp2((scores - largest) * SCALE)
                total = jnp.sum(weight, axis=1, keepdims=True) + total * shrink
                added = jnp.dot(
                    weight.astype(jnp.bfloat16),
                    gather(arrays, groups, window, rows, tokens, head),
                    preferred_element_type=jnp.float32,
                )
                result = (added + summed * shrink) / total
                write(head, tile, result.astype(jnp.bfloat16))
            return 0

        lax.fori_loop(0, heads, one_head, 0)


def attend(kernel, operands, outs, flops=0):
    return pl.pallas_call(
        kernel,
        out_shape=outs,
        in_specs=in_vmem(len(operands)),
        out_specs=in_vmem(len(outs)),
        compiler_params=pltpu.CompilerParams(vmem_limit_bytes=VMEM_LIMIT),
        cost_estimate=pl.CostEstimate(flops=flops, bytes_accessed=0, transcendentals=0),
    )(*operands)


def attend_early(queries, jobs, arrays, groups, tiles, tokens):
    outs = [
        pltpu.VMEM((len(heads) * tiles * len(layout) * tokens, HEAD_DIM), jnp.float32)
        for layout, heads in jobs
        for _ in range(3)
    ]
    kernel = functools.partial(
        early_body, groups, len(arrays), jobs, len(queries), tiles, tokens
    )
    return attend(kernel, [*queries, *arrays], outs, EARLY_FLOPS)


def attend_late(queries, layout, arrays, groups, tiles, tokens, heads, first, left, after):
    outs = [pltpu.VMEM((tiles * tokens, heads * HEAD_DIM), jnp.bfloat16)] * len(layout)
    sizes = (len(arrays), layout, len(queries), tiles, tokens, heads, first)
    kernel = functools.partial(late_body, groups, *sizes, len(left) // 3, len(after))
    return attend(kernel, [*queries, *arrays, *left, *after], outs)


def join_body(jobs, part, held, me_ref, *rest):
    out_ref, sems = rest[-2:]
    rest = rest[held:]
    me = me_ref[0]
    copies = []
    for i, (bit, base) in enumerate(jobs):
        lanes = pl.ds(pl.multiple_of((me ^ bit) * part + base, HEAD_DIM), rest[i].shape[1])
        copies.append(pltpu.make_async_copy(rest[i], out_ref.at[:, lanes], sems.at[i]))
    for copy in copies:
        copy.start()
    for copy in copies:
        copy.wait()


def join(me, pieces, rows, part, devices, begun=()):
    jobs = [piece[:2] for piece in pieces]
    hbm = [pl.BlockSpec(memory_space=pltpu.HBM)]
    return pl.pallas_call(
        functools.partial(join_body, jobs, part, len(begun)),
        out_shape=jax.ShapeDtypeStruct((rows, devices * part), jnp.bfloat16),
        in_specs=[pl.BlockSpec(memory_space=pltpu.SMEM)]
        + hbm * len(begun)
        + in_vmem(len(pieces)),
        out_specs=hbm[0],
        scratch_shapes=[pltpu.SemaphoreType.DMA((len(pieces),))],
        input_output_aliases={1: 0} if begun else {},
        compiler_params=pltpu.CompilerParams(vmem_limit_bytes=VMEM_LIMIT),
    )(me, *begun, *(piece[2] for piece in pieces))


def body(query, key, value, valid_rows):
    devices = lax.axis_size("head")
    columns = lax.axis_size("tok")
    height = columns // TIME_TILES
    tiles, tokens, width = query.shape
    heads = width // HEAD_DIM // devices
    me = lax.axis_index("head").astype(jnp.int32).reshape(1)
    flat = [field.reshape(tiles * tokens, width) for field in (query, key, value)]
    flat = [pltpu.with_memory_space_constraint(field, pltpu.HBM) for field in flat]
    own, sibling, passed, far = pack(me, valid_rows, flat, devices)
    rows = tiles * tokens

    def by_height(block):
        if height == 1:
            return [block]
        return [block] + [swap_pairs(block, phase, 1, height, columns) for phase in (0, 1)]

    def by_time(blocks):
        return [
            swap_pairs(b, phase, height, TIME_TILES, columns) for phase in (0, 1) for b in blocks
        ]

    sibling = swap_head(sibling, 1, devices)
    passed = swap_head(passed, 1, devices)
    far = [swap_head(b, bit, devices) for bit, b in enumerate(far, 2)]
    near = by_height(stack([own, sibling], [(0, own.shape[0]), (0, 2 * rows)]))
    near = near + by_time(near)

    unit = (heads + 2) * rows
    own_query, last = pack_last(me, flat, passed, devices)
    last = [swap_head(b, 2 * i + 2, devices) for i, b in enumerate(last)]
    queries = [own_query, sibling, *last]
    layout = [(0, 0, False), (1, 2 * rows, False)]
    layout += [(2 + bit // 2, bit % 2 * unit, True) for bit in range(devices - 2)]

    ends = [(bit // 2, bit % 2 * unit + heads * rows) for bit in range(devices - 2)]
    def sent(block):
        block = by_height(block)
        return block[1:] + by_time(block)

    first_heads, last_head = tuple(range(heads - 1)), (heads - 1,)
    across = sent(stack(far, [(0, 2 * rows)] * len(far), FIRST_FLOPS))
    near_groups = [(i, [[(i, 0, 0)], [(i, own.shape[0], 0)]]) for i in range(len(near))]
    own_fields = [[(len(near) + bit, 0, 0)] for bit in range(len(far))]
    groups = [(0, near_groups[0][1] + own_fields), *near_groups[1:]]
    close = attend_early(
        queries[:2], [(layout[:2], first_heads)], near + far, groups, tiles, tokens
    )

    spans = [(base, 2 * rows) for _, base in ends]
    across_last = sent(stack([last[i] for i, _ in ends], spans, after=close[:1]))
    for field, (i, base) in zip(own_fields, ends):
        field.append((len(near) + len(far) + i, base, heads - 1))
    jobs = [(layout[2:], first_heads), (layout, last_head)]
    groups = [(0, near_groups[0][1] + own_fields), *near_groups[1:]]
    left = attend_early(queries, jobs, near + far + last, groups, tiles, tokens)
    left = [[*close, *left[:3]], left[3:]]

    pieces = []
    for others, heads_now in ((across, first_heads), (across_last, last_head)):
        first = heads_now[0]
        groups = [
            (i, [[(len(others) + i, 2 * rows * bit, 0)] for bit in range(devices - 2)])
            for i in range(len(others))
        ]
        results = attend_late(
            queries,
            layout,
            near[1:] + others,
            groups,
            tiles,
            tokens,
            len(heads_now),
            first,
            left[len(pieces) > 0],
            [piece[2] for piece in pieces[:1]],
        )
        order = range(devices) if not pieces else range(devices - 1, -1, -1)
        pieces += [
            (bit, first * HEAD_DIM, swap_head(results[bit], bit, devices) if bit else results[0])
            for bit in order
        ]
    begun, ended = [], []
    for piece in pieces:
        (ended if piece[0] and piece[1] else begun).append(piece)
    shape = (rows, heads * HEAD_DIM, devices)
    joined = join(me, ended, *shape, [join(me, begun, *shape)])
    return joined.reshape(tiles, tokens, width)


def solution(mesh):
    placed = (
        P(("clips", "tok"), "head", None),
        P(("clips", "tok"), "head", None),
        P(("clips", "tok"), "head", None),
        P(("clips", "tok")),
    )
    return jax.shard_map(
        body,
        mesh=mesh,
        in_specs=placed,
        out_specs=P(("clips", "tok"), "head", None),
        check_vma=False,
    )
```

```python
import functools
import math

import jax
import jax.numpy as jnp
from jax import lax
from jax.experimental import pallas as pl
from jax.experimental.pallas import tpu as pltpu
from jax.sharding import PartitionSpec as P

HEAD_DIM = 128
TILE_H = 8
TILE_W = 8
TIME_TILES = 4
COUNT_ROWS = 16
MASKED = -1e30
LARGEST_TOTAL = 2.0**100
SCALE = math.log2(math.e) / math.sqrt(HEAD_DIM)
VMEM_LIMIT = 24 * 2**20
FIRST_FLOPS = 2500000000
EARLY_FLOPS = 0


def in_vmem(count):
    return [pl.BlockSpec(memory_space=pltpu.VMEM)] * count


def swap_head(block, bit, devices):
    return lax.ppermute(block, "head", [(i, i ^ bit) for i in range(devices)])


def swap_pairs(block, phase, stride, length, devices):
    route = []
    for i in range(devices):
        place = i // stride % length
        if place % 2 == phase and place + 1 < length:
            route += [(i, i + stride), (i + stride, i)]
    return lax.ppermute(block, "tok", route)


def lanes_of(owner, heads, first=0, count=None):
    start = pl.multiple_of((owner * heads + first) * HEAD_DIM, HEAD_DIM)
    return pl.ds(start, (heads if count is None else count) * HEAD_DIM)


def run_copies(jobs, sems):
    copies = [pltpu.make_async_copy(src, dst, sems.at[i]) for i, (src, dst) in enumerate(jobs)]
    for copy in copies:
        copy.start()
    return copies


def last_of(q_ref, k_ref, v_ref, owner, heads):
    sources = [q_ref.at[:, lanes_of(owner, heads, head, 1)] for head in range(heads)]
    return sources + [ref.at[:, lanes_of(owner, heads, heads - 1, 1)] for ref in (k_ref, v_ref)]


def pack_body(devices, heads, counts_in, me_ref, q_ref, k_ref, v_ref, *rest):
    own_ref, sibling_ref, passed_ref = rest[:3]
    far_refs = rest[3:-3]
    counts_ref, count_sem, sems = rest[-3:]
    rows = k_ref.shape[0]
    me = me_ref[0]
    count_copy = pltpu.make_async_copy(counts_in, counts_ref, count_sem)
    count_copy.start()
    beside = lanes_of(me ^ 1, heads)
    jobs = [
        (ref.at[:, beside], sibling_ref.at[pl.ds(i * rows, rows)])
        for i, ref in enumerate((k_ref, v_ref, q_ref))
    ]
    for bit, far_ref in enumerate(far_refs, 2):
        jobs += [
            (ref.at[:, lanes_of(me ^ bit, heads, 0, heads - 1)], far_ref.at[pl.ds(i * rows, rows)])
            for i, ref in enumerate((k_ref, v_ref))
        ]
    jobs += [
        (ref.at[:, lanes_of(me, heads)], own_ref.at[pl.ds(i * rows, rows)])
        for i, ref in enumerate((k_ref, v_ref))
    ]
    passed = [
        source
        for bit in range(3, devices, 2)
        for source in last_of(q_ref, k_ref, v_ref, me ^ bit, heads)
    ]
    jobs += [(source, passed_ref.at[pl.ds(i * rows, rows)]) for i, source in enumerate(passed)]
    copies = run_copies(jobs, sems)
    count_copy.wait()
    shape = (COUNT_ROWS, own_ref.shape[1])
    row = lax.broadcasted_iota(jnp.int32, shape, 0)
    filled = jnp.zeros(shape, jnp.float32)
    for tile in range(counts_ref.shape[0]):
        filled = jnp.where(row == tile, counts_ref[tile].astype(jnp.float32), filled)
    own_ref[pl.ds(2 * rows, COUNT_ROWS), :] = filled.astype(jnp.bfloat16)
    for copy in copies:
        copy.wait()


def pack(me, counts, fields, devices):
    rows, width = fields[0].shape
    part = width // devices
    heads = part // HEAD_DIM
    far = devices - 2
    shapes = [(2 * rows + COUNT_ROWS, part), (3 * rows, part)]
    shapes += [(far // 2 * (heads + 2) * rows, HEAD_DIM)] + [(2 * rows, part - HEAD_DIM)] * far
    results = pl.pallas_call(
        functools.partial(pack_body, devices, heads),
        out_shape=[pltpu.VMEM(shape, jnp.bfloat16) for shape in shapes],
        in_specs=[pl.BlockSpec(memory_space=pltpu.HBM), pl.BlockSpec(memory_space=pltpu.SMEM)]
        + [pl.BlockSpec(memory_space=pltpu.HBM)] * 3,
        out_specs=in_vmem(len(shapes)),
        scratch_shapes=[
            pltpu.SMEM(counts.shape, jnp.int32),
            pltpu.SemaphoreType.DMA,
            pltpu.SemaphoreType.DMA((5 + 2 * far + far // 2 * (heads + 2),)),
        ],
        compiler_params=pltpu.CompilerParams(vmem_limit_bytes=VMEM_LIMIT),
        cost_estimate=pl.CostEstimate(
            flops=0, bytes_accessed=12 * rows * width, transcendentals=0
        ),
    )(pltpu.with_memory_space_constraint(counts, pltpu.HBM), me, *fields)
    return results[0], results[1], results[2], results[3:]


def pack_last_body(devices, heads, me_ref, q_ref, k_ref, v_ref, passed_ref, *rest):
    own_q_ref, last_refs, sems = rest[0], rest[1:-1], rest[-1]
    rows = k_ref.shape[0]
    unit = (heads + 2) * rows
    me = me_ref[0]
    jobs = [(q_ref.at[:, lanes_of(me, heads)], own_q_ref)]
    for pair, last_ref in enumerate(last_refs):
        sources = last_of(q_ref, k_ref, v_ref, me ^ (2 * pair + 2), heads)
        jobs += [(source, last_ref.at[pl.ds(i * rows, rows)]) for i, source in enumerate(sources)]
        jobs.append((passed_ref.at[pl.ds(pair * unit, unit)], last_ref.at[pl.ds(unit, unit)]))
    for copy in run_copies(jobs, sems):
        copy.wait()


def pack_last(me, fields, passed, devices):
    rows, width = fields[0].shape
    part = width // devices
    heads = part // HEAD_DIM
    far = devices // 2 - 1
    shapes = [(rows, part)] + [(2 * (heads + 2) * rows, HEAD_DIM)] * far
    results = pl.pallas_call(
        functools.partial(pack_last_body, devices, heads),
        out_shape=[pltpu.VMEM(shape, jnp.bfloat16) for shape in shapes],
        in_specs=[pl.BlockSpec(memory_space=pltpu.SMEM)]
        + [pl.BlockSpec(memory_space=pltpu.HBM)] * 3
        + in_vmem(1),
        out_specs=in_vmem(len(shapes)),
        scratch_shapes=[pltpu.SemaphoreType.DMA((1 + far * (heads + 3),))],
        compiler_params=pltpu.CompilerParams(vmem_limit_bytes=VMEM_LIMIT),
        cost_estimate=pl.CostEstimate(
            flops=0, bytes_accessed=2 * (heads + 2) * rows * HEAD_DIM, transcendentals=0
        ),
    )(me, *fields, passed)
    return results[0], results[1:]


def stack_body(jobs, after, *refs):
    blocks, out_ref, sems = refs[: -2 - after], refs[-2], refs[-1]
    copies, base = [], 0
    for i, (first, size) in enumerate(jobs):
        source = blocks[i].at[pl.ds(first, size)]
        copies.append(
            pltpu.make_async_copy(source, out_ref.at[pl.ds(base, size)], sems.at[i])
        )
        base += size
    for copy in copies:
        copy.start()
    for copy in copies:
        copy.wait()


def stack(blocks, spans, flops=0, after=()):
    width = blocks[0].shape[1]
    rows = sum(size for _, size in spans)
    return pl.pallas_call(
        functools.partial(stack_body, spans, len(after)),
        out_shape=pltpu.VMEM((rows, width), jnp.bfloat16),
        in_specs=in_vmem(len(blocks) + len(after)),
        out_specs=pl.BlockSpec(memory_space=pltpu.VMEM),
        scratch_shapes=[pltpu.SemaphoreType.DMA((len(blocks),))],
        compiler_params=pltpu.CompilerParams(vmem_limit_bytes=VMEM_LIMIT),
        cost_estimate=pl.CostEstimate(
            flops=flops, bytes_accessed=rows * width, transcendentals=0
        ),
    )(*blocks, *after)


def features(head):
    return pl.ds(aligned(head * HEAD_DIM, HEAD_DIM), HEAD_DIM)


def window_of(tile, tiles, groups):
    near = range(max(tile - 1, 0), min(tile + 2, tiles))
    return [(group, other) for other in near for group in range(len(groups))]


def aligned(start, unit):
    return start if isinstance(start, int) else pl.multiple_of(start, unit)


def gather(arrays, groups, window, start, tokens, head):
    blocks = []
    for group, other in window:
        for field in groups[group][1]:
            index, base, first = field[0]
            for segment in field[1:]:
                if head >= segment[2]:
                    index, base, first = segment
            rows = pl.ds(base + start + other * tokens, tokens)
            blocks.append(arrays[index][rows, features(head - first)])
    return jnp.concatenate(blocks, 0)


def asked_of(queries, layout, head, tile, tokens, rows):
    blocks = []
    for index, base, by_rows in layout:
        if by_rows:
            at = pl.ds(aligned(base + head * rows + tile * tokens, tokens), tokens)
            blocks.append(queries[index][at, :])
        else:
            blocks.append(queries[index][pl.ds(base + tile * tokens, tokens), features(head)])
    return jnp.concatenate(blocks, 0)


def counts_of(arrays, groups, rows):
    counts = [arrays[i][pl.ds(2 * rows, COUNT_ROWS), pl.ds(0, HEAD_DIM)] for i, _ in groups]
    return [count.astype(jnp.float32) for count in counts]


def bias_of(counts, groups, window, tokens):
    lane = lax.broadcasted_iota(jnp.int32, (1, HEAD_DIM), 1)
    row = (lane // TILE_W % TILE_H).astype(jnp.float32)
    parts = []
    for group, other in window:
        part = jnp.where(row < counts[group][other : other + 1], 0.0, MASKED)
        parts += [part] * (len(groups[group][1]) * tokens // HEAD_DIM)
    return jnp.concatenate(parts, 1)


def products(queries, keys):
    return lax.dot_general(
        queries, keys, (((1,), (1,)), ((), ())), preferred_element_type=jnp.float32
    )


def early_body(groups, operands, jobs, asked, tiles, tokens, *refs):
    rows = tiles * tokens
    queries, arrays = refs[:asked], refs[asked : asked + operands]
    outs = refs[asked + operands :]
    counts = counts_of(arrays, groups, rows)
    windows = [window_of(tile, tiles, groups) for tile in range(tiles)]
    biases = [bias_of(counts, groups, window, tokens) for window in windows]

    def scored(job, head, tile):
        scores = products(
            asked_of(queries, jobs[job][0], head, tile, tokens, rows),
            gather(arrays, groups, windows[tile], 0, tokens, head),
        )
        scores = scores + biases[tile]
        return scores, jnp.max(scores, axis=1, keepdims=True)

    steps = [
        (job, head, tile)
        for job, (_, heads) in enumerate(jobs)
        for head in heads
        for tile in range(tiles)
    ]
    ahead = scored(*steps[0])
    for i, (job, head, tile) in enumerate(steps):
        scores, largest = ahead
        if i + 1 < len(steps):
            ahead = scored(*steps[i + 1])
        weight = jnp.exp2((scores - largest) * SCALE).astype(jnp.bfloat16)
        values = gather(arrays, groups, windows[tile], rows, tokens, head)
        values = jnp.concatenate([values, jnp.ones_like(values)], 1)
        summed = jnp.dot(weight, values, preferred_element_type=jnp.float32)
        layout, heads = jobs[job]
        block = len(layout) * tokens
        place = pl.ds(((head - heads[0]) * tiles + tile) * block, block)
        max_ref, total_ref, sum_ref = outs[3 * job : 3 * job + 3]
        max_ref[place, :] = jnp.broadcast_to(largest, (block, HEAD_DIM))
        sum_ref[place, :] = summed[:, :HEAD_DIM]
        total_ref[place, :] = summed[:, HEAD_DIM:]


def late_body(groups, operands, layout, asked, tiles, tokens, heads, first, parts, after, *refs):
    rows = tiles * tokens
    queries, arrays = refs[:asked], refs[asked : asked + operands]
    left = refs[asked + operands : asked + operands + 3 * parts]
    outs = refs[asked + operands + 3 * parts + after :]
    counts = counts_of(arrays, groups, rows)
    windows = [window_of(tile, tiles, groups) for tile in range(tiles)]
    block = len(layout) * tokens

    def scored(head, tile):
        return products(
            asked_of(queries, layout, first + head, tile, tokens, rows),
            gather(arrays, groups, windows[tile], 0, tokens, head),
        )

    def early(head, tile):
        share = block // parts
        at = pl.ds(aligned((head * tiles + tile) * share, share), share)
        return [jnp.concatenate([ref[at, :] for ref in left[which::3]], 0) for which in range(3)]

    def write(head, tile, result):
        for frame in range(len(layout)):
            outs[frame][pl.ds(tile * tokens, tokens), features(head)] = result[
                frame * tokens : (frame + 1) * tokens
            ]

    token = lax.broadcasted_iota(jnp.int32, (tokens, HEAD_DIM), 0)
    row = (token // TILE_W % TILE_H).astype(jnp.float32)
    real = [
        [jnp.where(row < count[n : n + 1], 1.0, 0.0).astype(jnp.bfloat16) for n in range(tiles)]
        for count in counts
    ]
    worst = jnp.zeros((block, HEAD_DIM), jnp.float32)
    steps = [(head, tile) for head in range(heads) for tile in range(tiles)]
    ahead = scored(*steps[0])
    for i, (head, tile) in enumerate(steps):
        scores, window = ahead, windows[tile]
        if i + 1 < len(steps):
            ahead = scored(*steps[i + 1])
        largest, total, summed = early(head, tile)
        largest = jnp.concatenate([largest] * (scores.shape[1] // HEAD_DIM), 1)
        weight = jnp.exp2((scores - largest) * SCALE).astype(jnp.bfloat16)
        kept = jnp.concatenate(
            [real[group][n] for group, n in window for _ in groups[group][1]], 0
        )
        values = gather(arrays, groups, window, rows, tokens, head) * kept
        added = jnp.dot(
            weight,
            jnp.concatenate([values, kept], 1),
            preferred_element_type=jnp.float32,
        )
        total = total + added[:, HEAD_DIM:]
        worst = jnp.where(total < LARGEST_TOTAL, worst, 1.0)
        result = (summed + added[:, :HEAD_DIM]) / total
        write(head, tile, result.astype(jnp.bfloat16))

    @pl.when(jnp.max(worst) > 0.0)
    def _():
        def one_head(head, _):
            for tile, window in enumerate(windows):
                before, total, summed = early(head, tile)
                scores = scored(head, tile) + bias_of(counts, groups, window, tokens)
                largest = jnp.maximum(before[:, :1], jnp.max(scores, axis=1, keepdims=True))
                shrink = jnp.exp2((before - largest) * SCALE)
                weight = jnp.exp2((scores - largest) * SCALE)
                total = jnp.sum(weight, axis=1, keepdims=True) + total * shrink
                added = jnp.dot(
                    weight.astype(jnp.bfloat16),
                    gather(arrays, groups, window, rows, tokens, head),
                    preferred_element_type=jnp.float32,
                )
                result = (added + summed * shrink) / total
                write(head, tile, result.astype(jnp.bfloat16))
            return 0

        lax.fori_loop(0, heads, one_head, 0)


def attend(kernel, operands, outs, flops=0):
    return pl.pallas_call(
        kernel,
        out_shape=outs,
        in_specs=in_vmem(len(operands)),
        out_specs=in_vmem(len(outs)),
        compiler_params=pltpu.CompilerParams(vmem_limit_bytes=VMEM_LIMIT),
        cost_estimate=pl.CostEstimate(flops=flops, bytes_accessed=0, transcendentals=0),
    )(*operands)


def attend_early(queries, jobs, arrays, groups, tiles, tokens):
    outs = [
        pltpu.VMEM((len(heads) * tiles * len(layout) * tokens, HEAD_DIM), jnp.float32)
        for layout, heads in jobs
        for _ in range(3)
    ]
    kernel = functools.partial(
        early_body, groups, len(arrays), jobs, len(queries), tiles, tokens
    )
    return attend(kernel, [*queries, *arrays], outs, EARLY_FLOPS)


def attend_late(queries, layout, arrays, groups, tiles, tokens, heads, first, left, after):
    outs = [pltpu.VMEM((tiles * tokens, heads * HEAD_DIM), jnp.bfloat16)] * len(layout)
    sizes = (len(arrays), layout, len(queries), tiles, tokens, heads, first)
    kernel = functools.partial(late_body, groups, *sizes, len(left) // 3, len(after))
    return attend(kernel, [*queries, *arrays, *left, *after], outs)


def join_body(jobs, part, held, me_ref, *rest):
    out_ref, sems = rest[-2:]
    rest = rest[held:]
    me = me_ref[0]
    copies = []
    for i, (bit, base) in enumerate(jobs):
        lanes = pl.ds(pl.multiple_of((me ^ bit) * part + base, HEAD_DIM), rest[i].shape[1])
        copies.append(pltpu.make_async_copy(rest[i], out_ref.at[:, lanes], sems.at[i]))
    for copy in copies:
        copy.start()
    for copy in copies:
        copy.wait()


def join(me, pieces, rows, part, devices, begun=()):
    jobs = [piece[:2] for piece in pieces]
    hbm = [pl.BlockSpec(memory_space=pltpu.HBM)]
    return pl.pallas_call(
        functools.partial(join_body, jobs, part, len(begun)),
        out_shape=jax.ShapeDtypeStruct((rows, devices * part), jnp.bfloat16),
        in_specs=[pl.BlockSpec(memory_space=pltpu.SMEM)]
        + hbm * len(begun)
        + in_vmem(len(pieces)),
        out_specs=hbm[0],
        scratch_shapes=[pltpu.SemaphoreType.DMA((len(pieces),))],
        input_output_aliases={1: 0} if begun else {},
        compiler_params=pltpu.CompilerParams(vmem_limit_bytes=VMEM_LIMIT),
    )(me, *begun, *(piece[2] for piece in pieces))


def body(query, key, value, valid_rows):
    devices = lax.axis_size("head")
    columns = lax.axis_size("tok")
    height = columns // TIME_TILES
    tiles, tokens, width = query.shape
    heads = width // HEAD_DIM // devices
    me = lax.axis_index("head").astype(jnp.int32).reshape(1)
    flat = [field.reshape(tiles * tokens, width) for field in (query, key, value)]
    flat = [pltpu.with_memory_space_constraint(field, pltpu.HBM) for field in flat]
    own, sibling, passed, far = pack(me, valid_rows, flat, devices)
    rows = tiles * tokens

    def by_height(block):
        if height == 1:
            return [block]
        return [block] + [swap_pairs(block, phase, 1, height, columns) for phase in (0, 1)]

    def by_time(blocks):
        return [
            swap_pairs(b, phase, height, TIME_TILES, columns) for phase in (0, 1) for b in blocks
        ]

    sibling = swap_head(sibling, 1, devices)
    passed = swap_head(passed, 1, devices)
    far = [swap_head(b, bit, devices) for bit, b in enumerate(far, 2)]
    near = by_height(stack([own, sibling], [(0, own.shape[0]), (0, 2 * rows)]))
    near = near + by_time(near)

    unit = (heads + 2) * rows
    own_query, last = pack_last(me, flat, passed, devices)
    last = [swap_head(b, 2 * i + 2, devices) for i, b in enumerate(last)]
    queries = [own_query, sibling, *last]
    layout = [(0, 0, False), (1, 2 * rows, False)]
    layout += [(2 + bit // 2, bit % 2 * unit, True) for bit in range(devices - 2)]

    ends = [(bit // 2, bit % 2 * unit + heads * rows) for bit in range(devices - 2)]
    def sent(block):
        block = by_height(block)
        return block[1:] + by_time(block)

    first_heads, last_head = tuple(range(heads - 1)), (heads - 1,)
    across = sent(stack(far, [(0, 2 * rows)] * len(far), FIRST_FLOPS))
    near_groups = [(i, [[(i, 0, 0)], [(i, own.shape[0], 0)]]) for i in range(len(near))]
    own_fields = [[(len(near) + bit, 0, 0)] for bit in range(len(far))]
    groups = [(0, near_groups[0][1] + own_fields), *near_groups[1:]]
    close = attend_early(
        queries[:2], [(layout[:2], first_heads)], near + far, groups, tiles, tokens
    )

    spans = [(base, 2 * rows) for _, base in ends]
    across_last = sent(stack([last[i] for i, _ in ends], spans, after=close[:1]))
    for field, (i, base) in zip(own_fields, ends):
        field.append((len(near) + len(far) + i, base, heads - 1))
    jobs = [(layout[2:], first_heads), (layout[:2], last_head), (layout[2:], last_head)]
    groups = [(0, near_groups[0][1] + own_fields), *near_groups[1:]]
    left = attend_early(queries, jobs, near + far + last, groups, tiles, tokens)
    left = [[*close, *left[:3]], left[3:]]

    pieces, after = [], []
    rounds = [
        (across, first_heads, range(2, devices), left[0][3:]),
        (across, first_heads, range(2), left[0][:3]),
        (across_last, last_head, range(2, devices), left[1][3:]),
        (across_last, last_head, range(2), left[1][:3]),
    ]
    for others, heads_now, frames, before in rounds:
        first = heads_now[0]
        groups = [
            (i, [[(len(others) + i, 2 * rows * bit, 0)] for bit in range(devices - 2)])
            for i in range(len(others))
        ]
        results = attend_late(
            queries,
            [layout[frame] for frame in frames],
            near[1:] + others,
            groups,
            tiles,
            tokens,
            len(heads_now),
            first,
            before,
            after,
        )
        after = [results[0]]
        found = list(zip(frames, results))
        pieces += [
            (bit, first * HEAD_DIM, swap_head(b, bit, devices) if bit else b)
            for bit, b in (found[::-1] if first else found)
        ]
    begun, ended = [], []
    for piece in pieces:
        (ended if piece[0] and piece[1] else begun).append(piece)
    shape = (rows, heads * HEAD_DIM, devices)
    joined = join(me, ended, *shape, [join(me, begun, *shape)])
    return joined.reshape(tiles, tokens, width)


def solution(mesh):
    placed = (
        P(("clips", "tok"), "head", None),
        P(("clips", "tok"), "head", None),
        P(("clips", "tok"), "head", None),
        P(("clips", "tok")),
    )
    return jax.shard_map(
        body,
        mesh=mesh,
        in_specs=placed,
        out_specs=P(("clips", "tok"), "head", None),
        check_vma=False,
    )
```
